256 devices in a mesh: dp: 32 (over z_hi, x, core), rep: 8 (over z_lo, y).
Axes of the slice: x: 4, y: 4, z: 8 (z_hi: 4, z_lo: 2; z = z_hi * 2 + z_lo), core: 2. Of those that a mesh axis runs over, the one named last changes fastest.
Arguments:
- images: bfloat16 [1536, 14, 14, 256], P(('dp', 'rep')), may hold values from -6 to 6
- labels: int32 [1536], P(('dp', 'rep')), may hold values from 0 to 2047
- conv_one: bfloat16 [3, 3, 256, 256], replicated, may hold values from -0.125 to 0.125
- conv_two: bfloat16 [3, 3, 256, 256], replicated, may hold values from -0.125 to 0.125
- prelu_slope: float32 [256], replicated, may hold values from 0.05 to 0.5
- spatial: float32 [196, 256], replicated, may hold values from -0.4375 to 0.4375
- head_weight: bfloat16 [256, 512], replicated, may hold values from -0.375 to 0.375
- class_queue: bfloat16 [2048, 512], replicated, may hold values from -6 to 6
- candidates: bfloat16 [16384, 512], P(('dp', 'rep')), may hold values from -6 to 6
- generator: int32 [32], replicated, may hold values from 0 to 31, each once
- offset: int32 [1], replicated, may hold values from 0 to 2047
Outputs:
- image_loss: float32 [1536], P(('dp', 'rep'))
- fresh_queue: bfloat16 [2048, 512], replicated
- update: float32 [1310720], P(('dp', 'rep'))
The draws below stay inside these ranges and needn't reach their ends.
Inputs may be any that keep to these rules, and one draw needn't show every extreme that they name: `generator`: each group index appears exactly once.
All inputs are finite; a program needn't handle non-finite values.
Results may differ from the reference program's by a relative error of at most 0.0054.
Values may be sent and summed in bfloat16 or wider, within the bound.
A program may use at most 128 MiB of HBM per device.

```python
import jax
import jax.numpy as jnp
from jax import lax

C = 256
E = 512
SIDE = 14
IMG_DEV = 6
QUEUE = 2048
GEN = 512
IMAGES = 1536
PARAMS = 1310720
N_DP = 32


def with_ends(drawn, rng, smallest, largest):
    shape = drawn.shape
    spot = [jax.random.randint(jax.random.fold_in(rng, axis), (), 0, shape[axis]) for axis in range(len(shape))]
    drawn = drawn.at[tuple(spot)].set(smallest)
    longest = shape.index(max(shape))
    spot[longest] = (spot[longest] + 1) % shape[longest]
    return drawn.at[tuple(spot)].set(largest)


def steps_of(stream_key, shape, shards, least, largest):
    loudness = 1.0
    for axis_at, blocks in shards:
        steps = jax.random.uniform(jax.random.fold_in(jax.random.fold_in(stream_key, 6), axis_at), (blocks,), jnp.float32, least / len(shards), largest / len(shards))
        loudness = loudness * jnp.repeat(jnp.exp(steps), shape[axis_at] // blocks).reshape((-1,) + (1,) * (len(shape) - 1 - axis_at))
    return loudness


def bell_draw(stream_key, dims, scale, bound, split=(), kind=jnp.bfloat16):
    loudness = steps_of(stream_key, dims, split, -0.22, 0.18) if split else 1.0
    drawn = jax.random.normal(stream_key, dims, jnp.float32) * scale * loudness
    return jnp.minimum(jnp.maximum(drawn, -bound), bound).astype(kind)


def setup_inputs(seed: int = 0) -> dict:
    splits = jax.random.split(jax.random.key(seed), 12)
    return {
        "images": bell_draw(splits[0], (IMAGES, SIDE, SIDE, C), 1.0, 6.0, ((0, 256),)),
        "labels": with_ends(jax.random.randint(splits[1], (IMAGES,), 0, QUEUE), jax.random.fold_in(splits[1], 1), 0, QUEUE - 1).astype(jnp.int32),
        "conv_one": bell_draw(splits[2], (3, 3, C, C), (9 * C) ** -0.5, 0.125),
        "conv_two": bell_draw(splits[3], (3, 3, C, C), (9 * C) ** -0.5, 0.125),
        "prelu_slope": jnp.clip(jax.random.uniform(splits[4], (C,), jnp.float32, 0.05, 0.5), 0.05, 0.5),
        "spatial": bell_draw(splits[5], (SIDE * SIDE, C), (SIDE * SIDE) ** -0.5, 0.4375, (), jnp.float32),
        "head_weight": bell_draw(splits[6], (C, E), C ** -0.5, 0.375),
        "class_queue": bell_draw(splits[7], (QUEUE, E), 1.0, 6.0),
        "candidates": bell_draw(splits[8], (GEN * N_DP, E), 1.0, 6.0, ((0, 256),)),
        "generator": jax.random.permutation(splits[9], N_DP).astype(jnp.int32),
        "offset": jax.random.randint(splits[10], (1,), 0, QUEUE).astype(jnp.int32),
    }


def patches_of(field):
    side_len = field.shape[1]
    padded = jnp.pad(field, ((0, 0), (1, 1), (1, 1), (0, 0)))
    shifted = [padded[:, row_shift:row_shift + side_len, col_shift:col_shift + side_len, :] for row_shift in range(3) for col_shift in range(3)]
    return jnp.concatenate(shifted, axis=3)

def fold_back(grad_patch, channels):
    image_count, side_len = (grad_patch.shape[0], grad_patch.shape[1])
    accum = jnp.zeros((image_count, side_len + 2, side_len + 2, channels), jnp.float32)
    for tap_index in range(9):
        row_shift, col_shift = (tap_index // 3, tap_index % 3)
        tap_block = grad_patch[..., tap_index * channels:(tap_index + 1) * channels]
        accum = accum + jnp.pad(tap_block, ((0, 0), (row_shift, 2 - row_shift), (col_shift, 2 - col_shift), (0, 0)))
    return accum[:, 1:-1, 1:-1, :]

def refresh(class_queue, class_panel, start_slot):
    rolled = jnp.roll(class_queue, -start_slot, axis=0)
    rolled = jnp.concatenate([class_panel, rolled[class_panel.shape[0]:]], axis=0)
    return jnp.roll(rolled, start_slot, axis=0)

def unit_rows(fresh_queue):
    rows_f = fresh_queue.astype(jnp.float32)
    return rows_f * lax.rsqrt(lax.optimization_barrier(jnp.sum(rows_f * rows_f, axis=1, keepdims=True)) + 1e-06)

def local_step(images, labels, conv_one, conv_two, prelu_slope, spatial, head_weight, unit_queue):
    image_count, side_len, channels = (images.shape[0], images.shape[1], images.shape[3])
    cell_count = image_count * side_len * side_len
    highest = lax.Precision.HIGHEST
    w_one = conv_one.reshape(9 * channels, channels)
    w_two = conv_two.reshape(9 * channels, channels)
    patch_one = patches_of(images).reshape(cell_count, 9 * channels)
    pre_act = jnp.dot(patch_one, w_one, preferred_element_type=jnp.float32)
    hidden = jnp.where(pre_act > 0, pre_act, prelu_slope[None, :] * pre_act).astype(jnp.bfloat16)
    patch_two = patches_of(hidden.reshape(image_count, side_len, side_len, channels)).reshape(cell_count, 9 * channels)
    block_out = images.reshape(cell_count, channels).astype(jnp.float32) + jnp.dot(patch_two, w_two, preferred_element_type=jnp.float32)
    pooled = lax.optimization_barrier(jnp.sum(block_out.reshape(image_count, side_len * side_len, channels) * spatial[None], axis=1))
    head_f = head_weight.astype(jnp.float32)
    embed = jnp.dot(pooled, head_f, precision=highest)
    inv_len = lax.rsqrt(lax.optimization_barrier(jnp.sum(embed * embed, axis=1, keepdims=True)) + 1e-06)
    unit_embed = embed * inv_len
    slots = unit_queue.shape[0]
    onehot = (labels[:, None] == jnp.arange(slots, dtype=jnp.int32)[None, :]).astype(jnp.float32)
    cosine = jnp.dot(unit_embed, unit_queue.T, precision=highest)
    logits = 64.0 * (cosine - 0.4 * onehot)
    exps = jnp.exp(logits)
    exp_total = lax.optimization_barrier(jnp.sum(exps, axis=1, keepdims=True))
    image_loss = jnp.log(exp_total[:, 0]) - lax.optimization_barrier(jnp.sum(logits * onehot, axis=1))
    d_logits = exps / exp_total - onehot
    d_unit = 64.0 * jnp.dot(d_logits, unit_queue, precision=highest)
    d_embed = (d_unit - unit_embed * lax.optimization_barrier(jnp.sum(d_unit * unit_embed, axis=1, keepdims=True))) * inv_len
    grad_head = jnp.dot(pooled.T, d_embed, precision=highest)
    d_pooled = jnp.dot(d_embed, head_f.T, precision=highest)
    d_block = (d_pooled[:, None, :] * spatial[None]).astype(jnp.bfloat16).reshape(cell_count, channels)
    grad_two = jnp.dot(patch_two.T, d_block, preferred_element_type=jnp.float32)
    grad_patch = jnp.dot(d_block, w_two.T, preferred_element_type=jnp.float32).reshape(image_count, side_len, side_len, 9 * channels)
    d_hidden = fold_back(grad_patch, channels).reshape(cell_count, channels)
    d_pre = (d_hidden * jnp.where(pre_act > 0, 1.0, prelu_slope[None, :])).astype(jnp.bfloat16)
    grad_one = jnp.dot(patch_one.T, d_pre, preferred_element_type=jnp.float32)
    grad_flat = jnp.concatenate([grad_one.reshape(-1), grad_two.reshape(-1), grad_head.reshape(-1)])
    return (image_loss, grad_flat)

def normalize_update(summed, conv_len, head_len):
    segments = [summed[:conv_len], summed[conv_len:2 * conv_len], summed[2 * conv_len:]]
    scaled = [segment * jnp.sqrt(jnp.float32(segment.shape[0])) * lax.rsqrt(jnp.sum(segment * segment) + 1e-06) for segment in segments]
    return jnp.concatenate(scaled)

def reference(images, labels, conv_one, conv_two, prelu_slope, spatial, head_weight, class_queue, candidates, generator, offset):
    class_panel = lax.dynamic_slice_in_dim(candidates, (generator[0] * GEN).astype(jnp.int32), GEN, 0)
    fresh_queue = refresh(class_queue, class_panel, offset[0])
    unit_queue = unit_rows(fresh_queue)
    group_count = images.shape[0] // IMG_DEV
    grouped_images = images.reshape((group_count, IMG_DEV) + images.shape[1:])
    grouped_labels = labels.reshape(group_count, IMG_DEV)

    def micro_step(carry, inputs):
        image_loss, grad_flat = local_step(inputs[0], inputs[1], conv_one, conv_two, prelu_slope, spatial, head_weight, unit_queue)
        return (carry + grad_flat, image_loss)
    start_grad = jnp.zeros((PARAMS,), jnp.float32)
    summed, losses = lax.scan(micro_step, start_grad, (grouped_images, grouped_labels))
    update = normalize_update(summed, conv_one.size, head_weight.size)
    return (losses.reshape(-1), fresh_queue, update)
```

```python
import functools

import jax
import jax.numpy as jnp
from jax import lax
from jax.experimental import pallas as pl
from jax.experimental.pallas import tpu as pltpu
from jax.sharding import PartitionSpec as P

F32 = jnp.float32
BF16 = jnp.bfloat16
MESH = pl.DeviceIdType.MESH
VMEM = pltpu.VMEM
DMA = pltpu.SemaphoreType.DMA

IMG, SIDE, C, E = 6, 14, 256, 512
PAD = 16
CELLS = SIDE * PAD
TALL = 288
QUEUE, GEN = 2048, 512
ROWS = 5120
CONV_ROWS = 2304
CHUNK = 20

NN = (((1,), (0,)), ((), ()))
NT = (((1,), (1,)), ((), ()))
TN = (((0,), (0,)), ((), ()))


def dot(a, b, dims=NN):
    return lax.dot_general(a, b, dims, preferred_element_type=F32)


def place():
    dp, rep = lax.axis_index("dp"), lax.axis_index("rep")
    return dp // 8, (dp // 2) % 4, dp % 2, rep // 4, rep % 4


def peer(dz=0, dx=0, dc=0, dy=0, dlo=0):
    z_hi, x, core, z_lo, y = place()
    z = (z_hi * 2 + (z_lo + dlo) % 2 + dz) % 8
    x, y, core = (x + dx) % 4, (y + dy) % 4, (core + dc) % 2
    return ((z // 2) * 4 + x) * 2 + core, (z % 2) * 4 + y


def stack3(v):
    high = v.astype(BF16).astype(F32)
    rest = v - high
    mid = rest.astype(BF16).astype(F32)
    low = rest - mid
    return jnp.concatenate([high, mid, low, jnp.zeros_like(v)], axis=0).astype(BF16)


def dot3(v, b, dims=NN):
    n = v.shape[0]
    out = dot(stack3(v), b, dims)
    return out[:n] + out[n : 2 * n] + out[2 * n : 3 * n]


def row_lengths(rows):
    f = rows.astype(F32)
    sq = f * f
    high = sq.astype(BF16)
    low = (sq - high.astype(F32)).astype(BF16)
    ones = jnp.ones((16, rows.shape[1]), BF16)
    total = dot(ones, high, NT) + dot(ones, low, NT)
    return lax.rsqrt(total[:8] + 1e-06)


XY = [(dx, dy) for dx in range(4) for dy in range(4) if dx or dy]


def kernel(
    img_hbm,
    lab,
    one_hbm,
    two_hbm,
    slope,
    spatial,
    head,
    queue_hbm,
    cand,
    gen,
    off,
    loss_out,
    fresh_out,
    upd_out,
    img,
    w1,
    w2,
    w2t,
    qb,
    s1,
    s2,
    sd,
    sp,
    xt,
    ht,
    fac,
    spm,
    pooled,
    cm,
    c_rec,
    ch,
    x_rec,
    ch2,
    z_rec,
    half,
    pan,
    gb,
    r1,
    ta,
    tbf,
    tb,
    ra,
    rb,
    uaf,
    ua,
    ubf,
    ub,
    ra2,
    rb2,
    zsf,
    zs,
    zr,
    ns,
    nr1,
    nr2,
    nr3,
    ld_sem,
    pan_s,
    pan_r,
    core_s,
    core_r,
    grad_s,
    grad_r,
    z_s,
    z_r,
    n_s,
    n_r,
):
    z_hi, x_me, core, z_lo, y_me = place()
    dp, rep = lax.axis_index("dp"), lax.axis_index("rep")
    z_me = z_hi * 2 + z_lo
    first_row = (dp * 8 + rep) * CHUNK

    def remote(src, dst, s, r, to):
        return pltpu.make_async_remote_copy(
            src_ref=src,
            dst_ref=dst,
            send_sem=s,
            recv_sem=r,
            device_id=to,
            device_id_type=MESH,
        )

    loads = [
        pltpu.make_async_copy(a, b, ld_sem.at[k])
        for k, (a, b) in enumerate(
            [(img_hbm, img), (one_hbm, w1), (two_hbm, w2), (queue_hbm, qb)]
        )
    ]
    for cp in loads:
        cp.start()

    barrier = pltpu.get_barrier_semaphore()
    friends = [dict(dc=1)] + [dict(dx=a, dy=b) for a, b in XY]
    friends += [dict(dz=k) for k in range(1, 8)]
    friends += [dict(dlo=1, dy=k) for k in range(1, 4)]
    for f in friends:
        pl.semaphore_signal(barrier, inc=1, device_id=peer(**f), device_id_type=MESH)

    mine = jnp.where(gen[0] == dp, 1.0, 0.0)
    cm[...] = (cand[...].astype(F32) * mine).astype(BF16)
    for buf in (s1, s2, sd, sp):
        for b in range(IMG):
            buf[b, 0:16, :] = jnp.zeros((16, 3 * C), BF16)
            buf[b, 240:TALL, :] = jnp.zeros((TALL - 240, 3 * C), BF16)
    pooled[...] = jnp.zeros((8, C), F32)

    pl.semaphore_wait(barrier, len(friends))

    other_half = cm.at[pl.ds(pl.multiple_of((1 - core) * 32, 32), 32)]
    p_core = remote(other_half, c_rec, pan_s.at[0], pan_r.at[0], peer(dc=1))
    p_core.start()

    quarter = lax.broadcasted_iota(jnp.int32, (CELLS, C), 0) % PAD
    inside = quarter < SIDE

    def shifted(buf, b, v):
        buf[b, 16:240, 0:C] = pltpu.roll(v, 1, 0).astype(BF16)
        buf[b, 16:240, C : 2 * C] = v.astype(BF16)
        buf[b, 16:240, 2 * C : 3 * C] = pltpu.roll(v, CELLS - 1, 0).astype(BF16)

    def flip(buf, b, v):
        tall = jnp.concatenate([v, jnp.zeros((32, C), F32)], axis=0)
        buf[:, pl.ds(pl.multiple_of(b * 256, 256), 256)] = tall.T.astype(BF16)

    loads[0].wait()

    def prepare(b, _):
        v = img[b].astype(F32)
        v = jnp.concatenate([v, jnp.zeros((SIDE, PAD - SIDE, C), F32)], axis=1)
        v = v.reshape(CELLS, C)
        shifted(s1, b, v)
        flip(xt, b, v)
        return 0

    lax.fori_loop(0, IMG, prepare, 0)

    p_core.wait()
    own_half = cm[pl.ds(pl.multiple_of(core * 32, 32), 32)]
    ch[...] = (own_half.astype(F32) + c_rec[...].astype(F32)).astype(BF16)
    p_x = [
        remote(ch, x_rec.at[k - 1], pan_s.at[k], pan_r.at[k], peer(dx=k))
        for k in (1, 3, 2)
    ]
    for cp in p_x:
        cp.start()

    loads[1].wait()

    def conv(buf, w, b):
        out = dot(buf[b, 0:CELLS], w[0].reshape(3 * C, C))
        out += dot(buf[b, 16 : 16 + CELLS], w[1].reshape(3 * C, C))
        return out + dot(buf[b, 32 : 32 + CELLS], w[2].reshape(3 * C, C))

    def first(b, _):
        pre = conv(s1, w1, b)
        f = jnp.where(inside, jnp.where(pre > 0, 1.0, slope[...]), 0.0)
        fac[b] = f
        h = pre * f
        shifted(s2, b, h)
        flip(ht, b, h)
        return 0

    lax.fori_loop(0, IMG, first, 0)

    for cp in p_x:
        cp.wait()
    whole = ch[...].astype(F32)
    for k in range(3):
        whole += x_rec[k].astype(F32)
    ch2[...] = whole.astype(BF16)
    p_z = [
        remote(ch2, z_rec.at[k - 1], pan_s.at[3 + k], pan_r.at[3 + k], peer(dz=2 * k))
        for k in (1, 3, 2)
    ]
    for cp in p_z:
        cp.start()

    for p in range(SIDE):
        spm[1, p * PAD : p * PAD + SIDE, :] = spatial[p * SIDE : (p + 1) * SIDE, :]
        spm[1, p * PAD + SIDE : (p + 1) * PAD, :] = jnp.zeros((PAD - SIDE, C), F32)
    loads[2].wait()

    def second(b, _):
        out = conv(s2, w2, b) + s1[b, 16:240, C : 2 * C].astype(F32)
        pooled[pl.ds(b, 1), :] = jnp.sum(out * spm[1], axis=0, keepdims=True)
        return 0

    lax.fori_loop(0, IMG, second, 0)

    for cp in p_z:
        cp.wait()
    whole = ch2[...].astype(F32)
    for k in range(3):
        whole += z_rec[k].astype(F32)
    half[rep] = whole.astype(BF16)
    rep_moves = [(lo, dy) for lo in range(2) for dy in range(4) if lo or dy]
    p_rep = [
        remote(
            half.at[rep],
            half.at[rep],
            pan_s.at[7 + k],
            pan_r.at[7 + k],
            peer(dlo=lo, dy=dy),
        )
        for k, (lo, dy) in enumerate(rep_moves)
    ]
    for cp in p_rep:
        cp.start()

    spm[0] = pltpu.roll(spm[1], 1, 0)
    spm[2] = pltpu.roll(spm[1], CELLS - 1, 0)
    for r in range(3):
        for s in range(3):
            turned = w2[2 - r, 2 - s].astype(F32).T
            w2t[r, s] = turned.astype(BF16)

    po = pooled[...]
    embed = dot3(po, head[...])
    inv_len = lax.rsqrt(jnp.sum(embed * embed, axis=1, keepdims=True) + 1e-06)
    unit = embed * inv_len
    rows8 = lax.broadcasted_iota(jnp.int32, (8, 1), 0)
    labels = jnp.full((8, 1), -1, jnp.int32)
    for b in range(IMG):
        labels = jnp.where(rows8 == b, lab[b], labels)
    shift = off[0]

    loads[3].wait()

    def score(rows, slots, keep):
        scale = row_lengths(rows)
        hot = (labels == slots) & keep
        logits = 64.0 * (dot3(unit, rows, NT) * scale - jnp.where(hot, 0.4, 0.0))
        exps = jnp.where(keep, jnp.exp(logits), 0.0)
        total = jnp.sum(exps, axis=1, keepdims=True)
        at_label = jnp.sum(jnp.where(hot, logits, 0.0), axis=1, keepdims=True)
        pulls = jnp.concatenate([exps * scale, jnp.where(hot, scale, 0.0)], axis=0)
        return total, at_label, dot3(pulls, rows)

    total = jnp.zeros((8, 1), F32)
    at_label = jnp.zeros((8, 1), F32)
    pulled = jnp.zeros((16, E), F32)
    for k in range(4):
        rows = qb[k * 512 : (k + 1) * 512, :]
        slots = lax.broadcasted_iota(jnp.int32, (8, 512), 1) + k * 512
        fresh = ((slots - shift + QUEUE) & (QUEUE - 1)) < GEN
        t, a, u = score(rows, slots, jnp.logical_not(fresh))
        total, at_label, pulled = total + t, at_label + a, pulled + u

    for cp in p_rep:
        cp.wait()
    my_rows = pl.ds(pl.multiple_of(core * 32, 32), 32)
    pan[:, my_rows, :] = half[...]
    p_last = remote(half, pan.at[:, my_rows, :], pan_s.at[14], pan_r.at[14], peer(dc=1))
    p_last.start()
    p_last.wait()

    rows = pan[...].reshape(GEN, E)
    j = lax.broadcasted_iota(jnp.int32, (8, GEN), 1)
    t, a, u = score(rows, (j + shift) & (QUEUE - 1), j >= 0)
    total, at_label, pulled = total + t, at_label + a, pulled + u
    loss = jnp.log(total) - at_label
    lanes = lax.broadcasted_iota(jnp.int32, (8, 128), 1)
    rows128 = lax.broadcasted_iota(jnp.int32, (8, 128), 0)
    loss_out[...] = jnp.sum(
        jnp.where(lanes == rows128, loss, 0.0), axis=0, keepdims=True
    )
    d_unit = 64.0 * (pulled[0:8] / total - pulled[8:16])
    d_embed = (d_unit - unit * jnp.sum(d_unit * unit, axis=1, keepdims=True)) * inv_len
    d_embed = jnp.where(rows8 < IMG, d_embed, 0.0)
    d_pooled = dot3(d_embed, head[...], NT)

    for b in range(IMG):
        for s in range(3):
            sd[b, 16:240, s * C : (s + 1) * C] = (
                spm[s] * d_pooled[b : b + 1, :]
            ).astype(BF16)

    po_h = po.astype(BF16).astype(F32)
    de_h = d_embed.astype(BF16).astype(F32)
    left = jnp.concatenate([po_h, po_h, po - po_h, jnp.zeros_like(po)], axis=0)
    right = jnp.concatenate(
        [de_h, d_embed - de_h, de_h, jnp.zeros_like(d_embed)], axis=0
    )
    g_head = dot(left.T.astype(BF16), right.astype(BF16))
    zsf2 = tbf.reshape(1280, 128)
    for k in range(2):
        for h in range(2):
            zsf2[pl.ds(k * 512 + h, 256, stride=2), :] = g_head[
                :, h * 256 + k * 128 : h * 256 + (k + 1) * 128
            ]
    for k in range(2):
        gb[2 * CONV_ROWS :, k * 128 : (k + 1) * 128] = zsf2[
            k * 512 : (k + 1) * 512, :
        ].astype(BF16)

    def weight_grad(turned, buf, tap, base):
        r, s = 2 - tap // 3, 2 - tap % 3
        rows = buf[:, r * 16 : r * 16 + 256, s * C : (s + 1) * C].reshape(IMG * 256, C)
        gb[base + tap * 256 : base + (tap + 1) * 256, :] = dot(turned[...], rows).astype(
            BF16
        )

    def core_send(a):
        theirs = pl.ds(pl.multiple_of((2 * a + 1 - core) * 160, 32), 160)
        cp = remote(
            gb.at[theirs],
            r1.at[pl.ds(a * 160, 160)],
            core_s.at[a],
            core_r.at[a],
            peer(dc=1),
        )
        cp.start()
        return cp

    core_cps = [None] * 16
    for tap in range(9):
        weight_grad(ht, sd, tap, CONV_ROWS)
        for a in range(8, 16):
            if core_cps[a] is None and (a + 1) * 320 <= CONV_ROWS + (tap + 1) * 256:
                core_cps[a] = core_send(a)
    for a in range(8, 16):
        if core_cps[a] is None:
            core_cps[a] = core_send(a)

    def back(b, _):
        out = conv(sd, w2t, b) * fac[b]
        shifted(sp, b, out)
        return 0

    lax.fori_loop(0, IMG, back, 0)

    def after_core(g):
        for a in range(8 * g, 8 * g + 8):
            core_cps[a].wait()

        def add(i, _):
            a = 8 * g + i
            ours = pl.ds(pl.multiple_of((2 * a + core) * 160, 32), 160)
            v = gb[ours, :].astype(F32)
            v += r1[pl.ds(pl.multiple_of(a * 160, 32), 160), :].astype(F32)
            ta[a] = v[:, 0:128].astype(BF16)
            for lo in range(2):
                for y in range(4):
                    at = pl.multiple_of(i * 40, 8)
                    k = (lo * 4 + y) * CHUNK
                    tbf[y, pl.ds(at + lo * CHUNK, CHUNK), :] = v[k : k + CHUNK, 128:256]
            return 0

        lax.fori_loop(0, 8, add, 0)
        for y in range(4):
            tb[g, y] = tbf[y].astype(BF16)
        cps = []
        for k in (1, 3, 2):
            to = (x_me + k) % 4
            n = g * 9 + (k - 1) * 3
            for h in range(2):
                cps.append(
                    remote(
                        ta.at[8 * g + 4 * h + to],
                        ra.at[g, k - 1, h],
                        grad_s.at[n + h],
                        grad_r.at[n + h],
                        peer(dx=k),
                    )
                )
            cps.append(
                remote(
                    tb.at[g, (y_me + k) % 4],
                    rb.at[g, k - 1],
                    grad_s.at[n + 2],
                    grad_r.at[n + 2],
                    peer(dy=k),
                )
            )
        for cp in cps:
            cp.start()
        return cps

    def after_first(g, cps):
        for cp in cps:
            cp.wait()
        for h in range(2):
            v = ta[8 * g + 4 * h + x_me].astype(F32)
            for k in range(3):
                v += ra[g, k, h].astype(F32)
            for lo in range(2):
                for y in range(4):
                    k = (lo * 4 + y) * CHUNK
                    at = (h * 2 + lo) * CHUNK
                    uaf[y, at : at + CHUNK, :] = v[k : k + CHUNK]
        v = tb[g, y_me].astype(F32)
        for k in range(3):
            v += rb[g, k].astype(F32)
        for h in range(2):
            for x in range(4):
                k = (h * 4 + x) * 40
                ubf[x, h * 40 : h * 40 + 40, :] = v[k : k + 40]
        ua[g] = uaf[...].astype(BF16)
        ub[g] = ubf[...].astype(BF16)
        cps = []
        for k in (1, 3, 2):
            n = 18 + g * 6 + (k - 1) * 2
            cps.append(
                remote(
                    ua.at[g, (y_me + k) % 4],
                    ra2.at[g, k - 1],
                    grad_s.at[n],
                    grad_r.at[n],
                    peer(dy=k),
                )
            )
            cps.append(
                remote(
                    ub.at[g, (x_me + k) % 4],
                    rb2.at[g, k - 1],
                    grad_s.at[n + 1],
                    grad_r.at[n + 1],
                    peer(dx=k),
                )
            )
        for cp in cps:
            cp.start()
        return cps

    def after_second(g, cps):
        for cp in cps:
            cp.wait()
        for side, (own, rec) in enumerate(((ua[g, y_me], ra2), (ub[g, x_me], rb2))):
            v = own.astype(F32)
            for k in range(3):
                v += rec[g, k].astype(F32)
            for z in range(4):
                zsf[4 * g + z, side * CHUNK : (side + 1) * CHUNK, :] = v[
                    z * CHUNK : (z + 1) * CHUNK
                ]

    early = after_core(1)
    for tap in range(9):
        weight_grad(xt, sp, tap, 0)
        for a in range(8):
            done = (tap + 1) * 256 + (256 if tap == 8 else 0)
            if core_cps[a] is None and (a + 1) * 320 <= done:
                core_cps[a] = core_send(a)
    early = after_first(1, early)
    late = after_core(0)

    def renew(k, _):
        at = pl.ds(pl.multiple_of(k * 256, 256), 256)
        slot = lax.broadcasted_iota(jnp.int32, (256, GEN), 0) + k * 256
        source = (slot - shift + QUEUE) & (QUEUE - 1)
        pick = jnp.where(
            source == lax.broadcasted_iota(jnp.int32, (256, GEN), 1), 1.0, 0.0
        ).astype(BF16)
        new = dot(pick, pan[...].reshape(GEN, E))
        old = qb[at, :].astype(F32)
        qb[at, :] = jnp.where(source < GEN, new, old).astype(BF16)
        return 0

    lax.fori_loop(0, QUEUE // 256, renew, 0)
    store = pltpu.make_async_copy(qb, fresh_out, ld_sem.at[4])
    store.start()

    after_second(1, early)
    late = after_first(0, late)
    after_second(0, late)

    for z in range(8):
        zsf[z, 40:48, :] = jnp.zeros((8, 128), F32)
        zs[z] = zsf[z].astype(BF16)
    z_cps = [
        remote(zs.at[(z_me + k) % 8], zr.at[k - 1], z_s.at[k - 1], z_r.at[k - 1], peer(dz=k))
        for k in (1, 7, 2, 6, 3, 5, 4)
    ]
    for cp in z_cps:
        cp.start()
    for cp in z_cps:
        cp.wait()
    v = zsf[z_me]
    for k in range(7):
        v += zr[k].astype(F32)
    low, high = v[0:CHUNK], v[CHUNK : 2 * CHUNK]

    row = first_row + lax.broadcasted_iota(jnp.int32, (CHUNK, 128), 0)
    in_one = row < CONV_ROWS
    in_head = row >= 2 * CONV_ROWS
    in_two = jnp.logical_not(in_one | in_head)
    sq = low * low + high * high
    for k, m in enumerate((in_one, in_two, in_head)):
        ns[0, k : k + 1, :] = jnp.sum(jnp.where(m, sq, 0.0), axis=0, keepdims=True)
    ns[0, 3:8, :] = jnp.zeros((5, 128), F32)

    def gather_sums(level, dst, moves, base):
        cps = [
            remote(ns.at[level], dst.at[k], n_s.at[base + k], n_r.at[base + k], peer(**m))
            for k, m in enumerate(moves)
        ]
        for cp in cps:
            cp.start()
        for cp in cps:
            cp.wait()
        s = ns[level]
        for k in range(len(moves)):
            s += dst[k]
        return s

    ns[1] = gather_sums(0, nr1, [dict(dx=a, dy=b) for a, b in XY], 0)
    ns[2] = gather_sums(1, nr2, [dict(dz=k) for k in range(1, 8)], 15)
    s = gather_sums(2, nr3, [dict(dc=1)], 22)
    s = jnp.sum(s, axis=1, keepdims=True)
    scale = lax.rsqrt(s + 1e-06)
    conv_n, head_n = (9 * C * C) ** 0.5, (C * E) ** 0.5
    factor = jnp.where(
        in_one,
        scale[0:1] * conv_n,
        jnp.where(in_two, scale[1:2] * conv_n, scale[2:3] * head_n),
    )
    upd_out[pl.ds(0, CHUNK, stride=2), :] = low * factor
    upd_out[pl.ds(1, CHUNK, stride=2), :] = high * factor
    store.wait()


SCRATCH = [
    VMEM((IMG, SIDE, SIDE, C), BF16),
    VMEM((3, 3, C, C), BF16),
    VMEM((3, 3, C, C), BF16),
    VMEM((3, 3, C, C), BF16),
    VMEM((QUEUE, E), BF16),
    VMEM((IMG, TALL, 3 * C), BF16),
    VMEM((IMG, TALL, 3 * C), BF16),
    VMEM((IMG, TALL, 3 * C), BF16),
    VMEM((IMG, TALL, 3 * C), BF16),
    VMEM((C, IMG * 256), BF16),
    VMEM((C, IMG * 256), BF16),
    VMEM((IMG, CELLS, C), F32),
    VMEM((3, CELLS, C), F32),
    VMEM((8, C), F32),
    VMEM((64, E), BF16),
    VMEM((32, E), BF16),
    VMEM((32, E), BF16),
    VMEM((3, 32, E), BF16),
    VMEM((32, E), BF16),
    VMEM((3, 32, E), BF16),
    VMEM((8, 32, E), BF16),
    VMEM((8, 64, E), BF16),
    VMEM((ROWS, C), BF16),
    VMEM((ROWS // 2, C), BF16),
    VMEM((16, 160, 128), BF16),
    VMEM((4, 320, 128), F32),
    VMEM((2, 4, 320, 128), BF16),
    VMEM((2, 3, 2, 160, 128), BF16),
    VMEM((2, 3, 320, 128), BF16),
    VMEM((4, 80, 128), F32),
    VMEM((2, 4, 80, 128), BF16),
    VMEM((4, 80, 128), F32),
    VMEM((2, 4, 80, 128), BF16),
    VMEM((2, 3, 80, 128), BF16),
    VMEM((2, 3, 80, 128), BF16),
    VMEM((8, 48, 128), F32),
    VMEM((8, 48, 128), BF16),
    VMEM((7, 48, 128), BF16),
    VMEM((3, 8, 128), F32),
    VMEM((15, 8, 128), F32),
    VMEM((7, 8, 128), F32),
    VMEM((1, 8, 128), F32),
    DMA((5,)),
    DMA((15,)),
    DMA((15,)),
    DMA((16,)),
    DMA((16,)),
    DMA((30,)),
    DMA((30,)),
    DMA((7,)),
    DMA((7,)),
    DMA((23,)),
    DMA((23,)),
]


def shards(
    images,
    labels,
    conv_one,
    conv_two,
    prelu_slope,
    spatial,
    head_weight,
    class_queue,
    candidates,
    generator,
    offset,
):
    far = pl.BlockSpec(memory_space=pl.ANY)
    near = pl.BlockSpec(memory_space=pltpu.VMEM)
    scalar = pl.BlockSpec(memory_space=pltpu.SMEM)
    loss, fresh, update = pl.pallas_call(
        kernel,
        out_shape=(
            jax.ShapeDtypeStruct((1, 128), F32),
            jax.ShapeDtypeStruct((QUEUE, E), BF16),
            jax.ShapeDtypeStruct((2 * CHUNK, 128), F32),
        ),
        in_specs=[far, scalar, far, far, near, near, near, far, near, scalar, scalar],
        out_specs=(near, far, near),
        scratch_shapes=SCRATCH,
        name="whole_step",
        compiler_params=pltpu.CompilerParams(
            collective_id=0, has_side_effects=True, vmem_limit_bytes=56 << 20
        ),
    )(
        images,
        labels,
        conv_one,
        conv_two,
        prelu_slope.reshape(1, C),
        spatial,
        head_weight,
        class_queue,
        candidates,
        generator,
        offset,
    )
    return loss[0, :IMG], fresh, update.reshape(2 * CHUNK * 128)


def solution(mesh):
    in_specs = (
        P(("dp", "rep"), None, None, None),
        P(("dp", "rep")),
        P(),
        P(),
        P(),
        P(),
        P(),
        P(),
        P(("dp", "rep"), None),
        P(),
        P(),
    )
    out_specs = (P(("dp", "rep")), P(), P(("dp", "rep")))
    return jax.shard_map(
        shards, mesh=mesh, in_specs=in_specs, out_specs=out_specs, check_vma=False
    )
```

```python
import functools

import jax
import jax.numpy as jnp
from jax import lax
from jax.experimental import pallas as pl
from jax.experimental.pallas import tpu as pltpu
from jax.sharding import PartitionSpec as P

F32 = jnp.float32
BF16 = jnp.bfloat16
MESH = pl.DeviceIdType.MESH
VMEM = pltpu.VMEM
DMA = pltpu.SemaphoreType.DMA

IMG, SIDE, C, E = 6, 14, 256, 512
PAD = 16
CELLS = SIDE * PAD
TALL = 288
QUEUE, GEN = 2048, 512
ROWS = 5120
CONV_ROWS = 2304
CHUNK = 20

NN = (((1,), (0,)), ((), ()))
NT = (((1,), (1,)), ((), ()))
TN = (((0,), (0,)), ((), ()))


def dot(a, b, dims=NN):
    return lax.dot_general(a, b, dims, preferred_element_type=F32)


def place():
    dp, rep = lax.axis_index("dp"), lax.axis_index("rep")
    return dp // 8, (dp // 2) % 4, dp % 2, rep // 4, rep % 4


def peer(dz=0, dx=0, dc=0, dy=0, dlo=0):
    z_hi, x, core, z_lo, y = place()
    z = (z_hi * 2 + (z_lo + dlo) % 2 + dz) % 8
    x, y, core = (x + dx) % 4, (y + dy) % 4, (core + dc) % 2
    return ((z // 2) * 4 + x) * 2 + core, (z % 2) * 4 + y


def stack3(v):
    high = v.astype(BF16).astype(F32)
    rest = v - high
    mid = rest.astype(BF16).astype(F32)
    low = rest - mid
    return jnp.concatenate([high, mid, low, jnp.zeros_like(v)], axis=0).astype(BF16)


def dot3(v, b, dims=NN):
    n = v.shape[0]
    out = dot(stack3(v), b, dims)
    return out[:n] + out[n : 2 * n] + out[2 * n : 3 * n]


def row_lengths(rows):
    f = rows.astype(F32)
    sq = f * f
    high = sq.astype(BF16)
    low = (sq - high.astype(F32)).astype(BF16)
    ones = jnp.ones((16, rows.shape[1]), BF16)
    total = dot(ones, high, NT) + dot(ones, low, NT)
    return lax.rsqrt(total[:8] + 1e-06)


XY = [(dx, dy) for dx in range(4) for dy in range(4) if dx or dy]


def kernel(
    img_hbm,
    lab_hbm,
    one_hbm,
    two_hbm,
    slope_hbm,
    spatial_hbm,
    head_hbm,
    queue_hbm,
    cand_hbm,
    gen_hbm,
    off_hbm,
    loss_out,
    fresh_out,
    upd_out,
    lab,
    gen,
    off,
    slope,
    spatial,
    head,
    cand,
    img,
    w1,
    w2,
    w2t,
    qb,
    s1,
    s2,
    sd,
    sp,
    xt,
    ht,
    fac,
    spm,
    pooled,
    cm,
    c_rec,
    ch,
    x_rec,
    ch2,
    z_rec,
    half,
    pan,
    gb,
    r1,
    ta,
    tbf,
    tb,
    ra,
    uaf,
    ua,
    ubf,
    ub,
    ra2,
    zsf,
    zs,
    zr,
    ns,
    nr1,
    nr2,
    nr3,
    hgf,
    ld_sem,
    sem,
    rep_sem,
    core_sem,
    first_sem,
    second_sem,
):
    z_hi, x_me, core, z_lo, y_me = place()
    dp, rep = lax.axis_index("dp"), lax.axis_index("rep")
    z_me = z_hi * 2 + z_lo
    first_row = (dp * 8 + rep) * CHUNK

    def remote(src, dst, s, r, to):
        return pltpu.make_async_remote_copy(
            src_ref=src,
            dst_ref=dst,
            send_sem=s,
            recv_sem=r,
            device_id=to,
            device_id_type=MESH,
        )

    def wait_bytes(ref, sem):
        pltpu.make_async_copy(ref, ref, sem).wait()

    pairs = dict(
        cand=(cand_hbm, cand),
        gen=(gen_hbm, gen),
        img=(img_hbm, img),
        w1=(one_hbm, w1),
        slope=(slope_hbm, slope),
        w2=(two_hbm, w2),
        spatial=(spatial_hbm, spatial),
        head=(head_hbm, head),
        lab=(lab_hbm, lab),
        off=(off_hbm, off),
        queue=(queue_hbm, qb),
    )
    loads = {
        name: pltpu.make_async_copy(a, b, ld_sem.at[k])
        for k, (name, (a, b)) in enumerate(pairs.items())
    }
    for cp in loads.values():
        cp.start()

    barrier = pltpu.get_barrier_semaphore()
    friends = [dict(dc=1)] + [dict(dx=a, dy=b) for a, b in XY]
    friends += [dict(dz=k) for k in range(1, 8)]
    friends += [dict(dlo=1, dy=k) for k in range(1, 4)]
    for f in friends:
        pl.semaphore_signal(barrier, inc=1, device_id=peer(**f), device_id_type=MESH)

    loads["cand"].wait()
    loads["gen"].wait()
    mine = jnp.where(gen[0] == dp, 1.0, 0.0)
    cm[...] = (cand[...].astype(F32) * mine).astype(BF16)
    pl.semaphore_wait(barrier, len(friends))

    other_half = cm.at[pl.ds(pl.multiple_of((1 - core) * 32, 32), 32)]
    p_core = remote(other_half, c_rec, sem.at[0], sem.at[1], peer(dc=1))
    p_core.start()

    for buf in (s1, s2, sd, sp):
        for b in range(IMG):
            buf[b, 0:16, :] = jnp.zeros((16, 3 * C), BF16)
            buf[b, 240:TALL, :] = jnp.zeros((TALL - 240, 3 * C), BF16)
    pooled[...] = jnp.zeros((8, C), F32)
    uaf[...] = jnp.zeros((4, 48, 128), F32)
    ubf[...] = jnp.zeros((4, 48, 128), F32)
    zsf[...] = jnp.zeros((8, 48, 128), F32)

    quarter = lax.broadcasted_iota(jnp.int32, (2 * CELLS, C), 0) % PAD
    inside = quarter < SIDE

    def shifted(buf, b, v):
        before, after = pltpu.roll(v, 1, 0), pltpu.roll(v, 2 * CELLS - 1, 0)
        for k in range(2):
            part = slice(k * CELLS, (k + 1) * CELLS)
            buf[b + k, 16:240, 0:C] = before[part].astype(BF16)
            buf[b + k, 16:240, C : 2 * C] = v[part].astype(BF16)
            buf[b + k, 16:240, 2 * C : 3 * C] = after[part].astype(BF16)

    def flip(buf, b, v):
        for k in range(2):
            part = v[k * CELLS : (k + 1) * CELLS]
            tall = jnp.concatenate([part, jnp.zeros((32, C), F32)], axis=0)
            at = pl.ds(pl.multiple_of((b + k) * 256, 256), 256)
            buf[:, at] = tall.T.astype(BF16)

    loads["img"].wait()

    def prepare(i, _):
        b = 2 * i
        v = img[pl.ds(b, 2)].astype(F32)
        v = jnp.concatenate([v, jnp.zeros((2, SIDE, PAD - SIDE, C), F32)], axis=2)
        v = v.reshape(2 * CELLS, C)
        shifted(s1, b, v)
        flip(xt, b, v)
        return 0

    lax.fori_loop(0, IMG // 2, prepare, 0)

    p_core.wait_recv()
    own_half = cm[pl.ds(pl.multiple_of(core * 32, 32), 32)]
    ch[...] = (own_half.astype(F32) + c_rec[...].astype(F32)).astype(BF16)
    for k in (1, 3, 2):
        remote(ch, x_rec.at[k - 1], sem.at[2], sem.at[3], peer(dx=k)).start()

    loads["w1"].wait()
    loads["slope"].wait()

    def conv(buf, w, b):
        out = None
        for r in range(3):
            rows = buf[pl.ds(b, 2), r * 16 : r * 16 + CELLS, :]
            term = dot(rows.reshape(2 * CELLS, 3 * C), w[r].reshape(3 * C, C))
            out = term if out is None else out + term
        return out

    def first(i, _):
        b = 2 * i
        pre = conv(s1, w1, b)
        f = jnp.where(inside, jnp.where(pre > 0, 1.0, slope[...]), 0.0)
        fac[pl.ds(b, 2)] = f.reshape(2, CELLS, C)
        h = pre * f
        shifted(s2, b, h)
        flip(ht, b, h)
        return 0

    lax.fori_loop(0, IMG // 2, first, 0)

    wait_bytes(x_rec, sem.at[3])
    whole = ch[...].astype(F32)
    for k in range(3):
        whole += x_rec[k].astype(F32)
    ch2[...] = whole.astype(BF16)
    for k in (1, 3, 2):
        remote(ch2, z_rec.at[k - 1], sem.at[4], sem.at[5], peer(dz=2 * k)).start()

    loads["spatial"].wait()
    for p in range(SIDE):
        spm[1, p * PAD : p * PAD + SIDE, :] = spatial[p * SIDE : (p + 1) * SIDE, :]
        spm[1, p * PAD + SIDE : (p + 1) * PAD, :] = jnp.zeros((PAD - SIDE, C), F32)
    loads["w2"].wait()

    def second(i, _):
        b = 2 * i
        out = conv(s2, w2, b)
        for k in range(2):
            part = out[k * CELLS : (k + 1) * CELLS]
            part += s1[b + k, 16:240, C : 2 * C].astype(F32)
            pooled[pl.ds(b + k, 1), :] = jnp.sum(part * spm[1], axis=0, keepdims=True)
        return 0

    lax.fori_loop(0, IMG // 2, second, 0)

    wait_bytes(z_rec, sem.at[5])
    whole = ch2[...].astype(F32)
    for k in range(3):
        whole += z_rec[k].astype(F32)
    half[rep] = whole.astype(BF16)
    rep_moves = [(lo, dy) for lo in range(2) for dy in range(4) if lo or dy]
    for k, (lo, dy) in enumerate(rep_moves):
        to = peer(dlo=lo, dy=dy)
        remote(half.at[rep], half.at[rep], sem.at[6], rep_sem.at[k], to).start()

    spm[0] = pltpu.roll(spm[1], 1, 0)
    spm[2] = pltpu.roll(spm[1], CELLS - 1, 0)
    for r in range(3):
        for s in range(3):
            turned = w2[2 - r, 2 - s].astype(F32).T
            w2t[r, s] = turned.astype(BF16)

    for name in ("head", "lab", "off", "queue"):
        loads[name].wait()
    po = pooled[...]
    embed = dot3(po, head[...])
    inv_len = lax.rsqrt(jnp.sum(embed * embed, axis=1, keepdims=True) + 1e-06)
    unit = embed * inv_len
    rows8 = lax.broadcasted_iota(jnp.int32, (8, 1), 0)
    labels = jnp.full((8, 1), -1, jnp.int32)
    for b in range(IMG):
        labels = jnp.where(rows8 == b, lab[b], labels)
    shift = off[0]

    def score(rows, slots, keep):
        scale = row_lengths(rows)
        hot = (labels == slots) & keep
        logits = 64.0 * (dot3(unit, rows, NT) * scale - jnp.where(hot, 0.4, 0.0))
        exps = jnp.where(keep, jnp.exp(logits), 0.0)
        total = jnp.sum(exps, axis=1, keepdims=True)
        at_label = jnp.sum(jnp.where(hot, logits, 0.0), axis=1, keepdims=True)
        pulls = jnp.concatenate([exps * scale, jnp.where(hot, scale, 0.0)], axis=0)
        return total, at_label, dot3(pulls, rows)

    total = jnp.zeros((8, 1), F32)
    at_label = jnp.zeros((8, 1), F32)
    pulled = jnp.zeros((16, E), F32)
    for k in range(4):
        rows = qb[k * 512 : (k + 1) * 512, :]
        slots = lax.broadcasted_iota(jnp.int32, (8, 512), 1) + k * 512
        fresh = ((slots - shift + QUEUE) & (QUEUE - 1)) < GEN
        t, a, u = score(rows, slots, jnp.logical_not(fresh))
        total, at_label, pulled = total + t, at_label + a, pulled + u

    my_rows = pl.ds(pl.multiple_of(core * 32, 32), 32)

    other_rows = pl.ds(pl.multiple_of((1 - core) * 32, 32), 32)

    def pass_on(which):
        dst = pan.at[which, my_rows]
        remote(half.at[which], dst, sem.at[7], sem.at[8], peer(dc=1)).start()

    pass_on(rep)
    for k, (lo, dy) in enumerate(rep_moves):
        which = ((z_lo + lo) % 2) * 4 + (y_me - dy) % 4
        wait_bytes(half.at[which], rep_sem.at[k])
        pass_on(which)
    pan[:, my_rows, :] = half[...]
    wait_bytes(pan.at[:, other_rows], sem.at[8])

    rows = pan[...].reshape(GEN, E)
    j = lax.broadcasted_iota(jnp.int32, (8, GEN), 1)
    t, a, u = score(rows, (j + shift) & (QUEUE - 1), j >= 0)
    total, at_label, pulled = total + t, at_label + a, pulled + u
    loss = jnp.log(total) - at_label
    lanes = lax.broadcasted_iota(jnp.int32, (8, 128), 1)
    rows128 = lax.broadcasted_iota(jnp.int32, (8, 128), 0)
    loss_out[...] = jnp.sum(jnp.where(lanes == rows128, loss, 0.0), axis=0)[:IMG]
    d_unit = 64.0 * (pulled[0:8] / total - pulled[8:16])
    d_embed = (d_unit - unit * jnp.sum(d_unit * unit, axis=1, keepdims=True)) * inv_len
    d_embed = jnp.where(rows8 < IMG, d_embed, 0.0)
    d_pooled = dot3(d_embed, head[...], NT)

    for b in range(IMG):
        for s in range(3):
            sd[b, 16:240, s * C : (s + 1) * C] = (
                spm[s] * d_pooled[b : b + 1, :]
            ).astype(BF16)

    po_h = po.astype(BF16).astype(F32)
    de_h = d_embed.astype(BF16).astype(F32)
    left = jnp.concatenate([po_h, po_h, po - po_h, jnp.zeros_like(po)], axis=0)
    right = jnp.concatenate(
        [de_h, d_embed - de_h, de_h, jnp.zeros_like(d_embed)], axis=0
    )
    g_head = dot(left.T.astype(BF16), right.astype(BF16))
    zsf2 = hgf
    for k in range(2):
        for h in range(2):
            zsf2[pl.ds(k * 512 + h, 256, stride=2), :] = g_head[
                :, h * 256 + k * 128 : h * 256 + (k + 1) * 128
            ]
    for k in range(2):
        gb.reshape(ROWS, C)[2 * CONV_ROWS :, k * 128 : (k + 1) * 128] = zsf2[
            k * 512 : (k + 1) * 512, :
        ].astype(BF16)

    flat = gb.reshape(ROWS, C)

    def weight_grad(turned, buf, tap, base):
        r, s = 2 - tap // 3, 2 - tap % 3
        rows = buf[:, r * 16 : r * 16 + 256, s * C : (s + 1) * C].reshape(IMG * 256, C)
        flat[base + tap * 256 : base + (tap + 1) * 256, :] = dot(turned[...], rows).astype(
            BF16
        )

    def send(u, first, count):
        at = pl.ds(4 * u + first, count)
        src, dst = gb.at[at, 1 - core], r1.at[at]
        remote(src, dst, sem.at[9], core_sem.at[u], peer(dc=1)).start()

    def two(*taps):
        for tap in taps:
            weight_grad(ht, sd, tap, CONV_ROWS)

    def one(*taps):
        for tap in taps:
            weight_grad(xt, sp, tap, 0)

    def back(i, _):
        b = 2 * i
        out = conv(sd, w2t, b) * fac[pl.ds(b, 2)].reshape(2 * CELLS, C)
        shifted(sp, b, out)
        return 0

    def after_core(u):
        wait_bytes(r1.at[pl.ds(4 * u, 4)], core_sem.at[u])
        for x in range(4):
            a = 4 * u + x
            v = gb[a, core].astype(F32) + r1[a].astype(F32)
            ta[a] = v[:, 0:128].astype(BF16)
            for lo in range(2):
                for y in range(4):
                    k, at = (lo * 4 + y) * CHUNK, (x * 2 + lo) * CHUNK
                    tbf[y, at : at + CHUNK, :] = v[k : k + CHUNK, 128:256]
        tb[u] = tbf[...].astype(BF16)
        for k in (1, 3, 2):
            src = ta.at[4 * u + (x_me + k) % 4]
            remote(src, ra.at[u, k - 1], sem.at[10], first_sem.at[u], peer(dx=k)).start()
            src = tb.at[u, (y_me + k) % 4]
            remote(src, ra.at[u, k + 2], sem.at[10], first_sem.at[u], peer(dy=k)).start()

    def after_first(u):
        wait_bytes(ra.at[u], first_sem.at[u])
        v = ta[4 * u + x_me].astype(F32)
        for k in range(3):
            v += ra[u, k].astype(F32)
        for lo in range(2):
            for y in range(4):
                k, at = (lo * 4 + y) * CHUNK, lo * CHUNK
                uaf[y, at : at + CHUNK, :] = v[k : k + CHUNK]
        v = tb[u, y_me].astype(F32)
        for k in range(3):
            v += ra[u, k + 3].astype(F32)
        for x in range(4):
            ubf[x, 0:40, :] = v[x * 40 : (x + 1) * 40]
        ua[u] = uaf[...].astype(BF16)
        ub[u] = ubf[...].astype(BF16)
        for k in (1, 3, 2):
            src = ua.at[u, (y_me + k) % 4]
            remote(src, ra2.at[u, k - 1], sem.at[11], second_sem.at[u], peer(dy=k)).start()
            src = ub.at[u, (x_me + k) % 4]
            remote(src, ra2.at[u, k + 2], sem.at[11], second_sem.at[u], peer(dx=k)).start()

    def after_second(u):
        wait_bytes(ra2.at[u], second_sem.at[u])
        for side, own in enumerate((ua[u, y_me], ub[u, x_me])):
            v = own.astype(F32)
            for k in range(3):
                v += ra2[u, 3 * side + k].astype(F32)
            for lo in range(2):
                zsf[2 * u + lo, side * CHUNK : (side + 1) * CHUNK, :] = v[
                    lo * CHUNK : (lo + 1) * CHUNK
                ]

    def renew(k, _):
        at = pl.ds(pl.multiple_of(k * 256, 256), 256)
        slot = lax.broadcasted_iota(jnp.int32, (256, GEN), 0) + k * 256
        source = (slot - shift + QUEUE) & (QUEUE - 1)
        pick = jnp.where(
            source == lax.broadcasted_iota(jnp.int32, (256, GEN), 1), 1.0, 0.0
        ).astype(BF16)
        new = dot(pick, pan[...].reshape(GEN, E))
        old = qb[at, :].astype(F32)
        fresh_out[at, :] = jnp.where(source[:, 0:1] < GEN, new, old).astype(BF16)
        return 0

    two(6, 7, 8)
    send(3, 0, 4)
    two(1, 2, 3, 4, 5)
    send(2, 0, 4)
    two(0)
    lax.fori_loop(0, 1, back, 0)
    after_core(3)
    lax.fori_loop(1, IMG // 2, back, 0)
    after_core(2)
    one(5, 6, 7, 8)
    send(1, 0, 4)
    one(0, 1, 2)
    send(0, 0, 2)
    one(3, 4)
    send(0, 2, 2)
    after_core(1)
    after_core(0)
    after_first(3)
    after_first(2)
    lax.fori_loop(0, 4, renew, 0)
    after_first(1)
    after_first(0)
    lax.fori_loop(4, 8, renew, 0)
    after_second(3)
    after_second(2)
    after_second(1)
    after_second(0)

    for z in range(8):
        zs[z] = zsf[z].astype(BF16)
    for k in (1, 7, 2, 6, 3, 5, 4):
        src = zs.at[(z_me + k) % 8]
        remote(src, zr.at[k - 1], sem.at[12], sem.at[13], peer(dz=k)).start()
    wait_bytes(zr, sem.at[13])
    v = zsf[z_me]
    for k in range(7):
        v += zr[k].astype(F32)
    low, high = v[0:CHUNK], v[CHUNK : 2 * CHUNK]

    row = first_row + lax.broadcasted_iota(jnp.int32, (CHUNK, 128), 0)
    in_one = row < CONV_ROWS
    in_head = row >= 2 * CONV_ROWS
    in_two = jnp.logical_not(in_one | in_head)
    sq = low * low + high * high
    for k, m in enumerate((in_one, in_two, in_head)):
        ns[0, k : k + 1, :] = jnp.sum(jnp.where(m, sq, 0.0), axis=0, keepdims=True)
    ns[0, 3:8, :] = jnp.zeros((5, 128), F32)

    def gather_sums(level, dst, moves):
        there, here = sem.at[14 + 2 * level], sem.at[15 + 2 * level]
        for k, m in enumerate(moves):
            remote(ns.at[level], dst.at[k], there, here, peer(**m)).start()
        wait_bytes(dst, here)
        s = ns[level]
        for k in range(len(moves)):
            s += dst[k]
        return s

    ns[1] = gather_sums(0, nr1, [dict(dx=a, dy=b) for a, b in XY])
    ns[2] = gather_sums(1, nr2, [dict(dz=k) for k in range(1, 8)])
    s = gather_sums(2, nr3, [dict(dc=1)])
    s = jnp.sum(s, axis=1, keepdims=True)
    scale = lax.rsqrt(s + 1e-06)
    conv_n, head_n = (9 * C * C) ** 0.5, (C * E) ** 0.5
    factor = jnp.where(
        in_one,
        scale[0:1] * conv_n,
        jnp.where(in_two, scale[1:2] * conv_n, scale[2:3] * head_n),
    )
    upd_out[pl.ds(0, CHUNK, stride=2), :] = low * factor
    upd_out[pl.ds(1, CHUNK, stride=2), :] = high * factor

    p_core.wait_send()
    sent = [
        (x_rec, 2),
        (z_rec, 4),
        (half.at[pl.ds(0, 7)], 6),
        (half, 7),
        (r1, 9),
        (ra, 10),
        (ra2, 11),
        (zr, 12),
        (nr1, 14),
        (nr2, 16),
        (nr3, 18),
    ]
    for ref, k in sent:
        wait_bytes(ref, sem.at[k])


SCRATCH = [
    pltpu.SMEM((IMG,), jnp.int32),
    pltpu.SMEM((32,), jnp.int32),
    pltpu.SMEM((1,), jnp.int32),
    VMEM((1, C), F32),
    VMEM((SIDE * SIDE, C), F32),
    VMEM((C, E), BF16),
    VMEM((64, E), BF16),
    VMEM((IMG, SIDE, SIDE, C), BF16),
    VMEM((3, 3, C, C), BF16),
    VMEM((3, 3, C, C), BF16),
    VMEM((3, 3, C, C), BF16),
    VMEM((QUEUE, E), BF16),
    VMEM((IMG, TALL, 3 * C), BF16),
    VMEM((IMG, TALL, 3 * C), BF16),
    VMEM((IMG, TALL, 3 * C), BF16),
    VMEM((IMG, TALL, 3 * C), BF16),
    VMEM((C, IMG * 256), BF16),
    VMEM((C, IMG * 256), BF16),
    VMEM((IMG, CELLS, C), F32),
    VMEM((3, CELLS, C), F32),
    VMEM((8, C), F32),
    VMEM((64, E), BF16),
    VMEM((32, E), BF16),
    VMEM((32, E), BF16),
    VMEM((3, 32, E), BF16),
    VMEM((32, E), BF16),
    VMEM((3, 32, E), BF16),
    VMEM((8, 32, E), BF16),
    VMEM((8, 64, E), BF16),
    VMEM((16, 2, 160, C), BF16),
    VMEM((16, 160, C), BF16),
    VMEM((16, 160, 128), BF16),
    VMEM((4, 160, 128), F32),
    VMEM((4, 4, 160, 128), BF16),
    VMEM((4, 6, 160, 128), BF16),
    VMEM((4, 48, 128), F32),
    VMEM((4, 4, 48, 128), BF16),
    VMEM((4, 48, 128), F32),
    VMEM((4, 4, 48, 128), BF16),
    VMEM((4, 6, 48, 128), BF16),
    VMEM((8, 48, 128), F32),
    VMEM((8, 48, 128), BF16),
    VMEM((7, 48, 128), BF16),
    VMEM((3, 8, 128), F32),
    VMEM((15, 8, 128), F32),
    VMEM((7, 8, 128), F32),
    VMEM((1, 8, 128), F32),
    VMEM((1024, 128), F32),
    DMA((11,)),
    DMA((20,)),
    DMA((7,)),
    DMA((4,)),
    DMA((4,)),
    DMA((4,)),
]


def shards(
    images,
    labels,
    conv_one,
    conv_two,
    prelu_slope,
    spatial,
    head_weight,
    class_queue,
    candidates,
    generator,
    offset,
):
    far = pl.BlockSpec(memory_space=pl.ANY)
    near = pl.BlockSpec(memory_space=pltpu.VMEM)
    loss, fresh, update = pl.pallas_call(
        kernel,
        out_shape=(
            VMEM((IMG,), F32),
            VMEM((QUEUE, E), BF16),
            VMEM((2 * CHUNK, 128), F32),
        ),
        in_specs=[far] * 11,
        out_specs=(near, near, near),
        scratch_shapes=SCRATCH,
        name="whole_step",
        compiler_params=pltpu.CompilerParams(
            collective_id=0, has_side_effects=True, vmem_limit_bytes=56 << 20
        ),
    )(
        images,
        labels,
        conv_one,
        conv_two,
        prelu_slope.reshape(1, C),
        spatial,
        head_weight,
        class_queue,
        candidates,
        generator,
        offset,
    )
    return loss, fresh, update.reshape(2 * CHUNK * 128)


def solution(mesh):
    in_specs = (
        P(("dp", "rep"), None, None, None),
        P(("dp", "rep")),
        P(),
        P(),
        P(),
        P(),
        P(),
        P(),
        P(("dp", "rep"), None),
        P(),
        P(),
    )
    out_specs = (P(("dp", "rep")), P(), P(("dp", "rep")))
    return jax.shard_map(
        shards, mesh=mesh, in_specs=in_specs, out_specs=out_specs, check_vma=False
    )
```

```python
import functools

import jax
import jax.numpy as jnp
from jax import lax
from jax.experimental import pallas as pl
from jax.experimental.pallas import tpu as pltpu
from jax.sharding import PartitionSpec as P

F32 = jnp.float32
BF16 = jnp.bfloat16
MESH = pl.DeviceIdType.MESH
VMEM = pltpu.VMEM
DMA = pltpu.SemaphoreType.DMA

IMG, SIDE, C, E = 6, 14, 256, 512
PAD = 16
CELLS = SIDE * PAD
TALL = 288
QUEUE, GEN = 2048, 512
ROWS = 5120
CONV_ROWS = 2304
CHUNK = 20

NN = (((1,), (0,)), ((), ()))
NT = (((1,), (1,)), ((), ()))
TN = (((0,), (0,)), ((), ()))


def dot(a, b, dims=NN):
    return lax.dot_general(a, b, dims, preferred_element_type=F32)


def place():
    dp, rep = lax.axis_index("dp"), lax.axis_index("rep")
    return dp // 8, (dp // 2) % 4, dp % 2, rep // 4, rep % 4


def peer(dz=0, dx=0, dc=0, dy=0, dlo=0):
    z_hi, x, core, z_lo, y = place()
    z = (z_hi * 2 + (z_lo + dlo) % 2 + dz) % 8
    x, y, core = (x + dx) % 4, (y + dy) % 4, (core + dc) % 2
    return ((z // 2) * 4 + x) * 2 + core, (z % 2) * 4 + y


def stack3(v):
    high = v.astype(BF16).astype(F32)
    rest = v - high
    mid = rest.astype(BF16).astype(F32)
    low = rest - mid
    return jnp.concatenate([high, mid, low, jnp.zeros_like(v)], axis=0).astype(BF16)


def dot3(v, b, dims=NN):
    n = v.shape[0]
    out = dot(stack3(v), b, dims)
    return out[:n] + out[n : 2 * n] + out[2 * n : 3 * n]


def row_lengths(rows):
    f = rows.astype(F32)
    sq = f * f
    high = sq.astype(BF16)
    low = (sq - high.astype(F32)).astype(BF16)
    ones = jnp.ones((16, rows.shape[1]), BF16)
    total = dot(ones, high, NT) + dot(ones, low, NT)
    return lax.rsqrt(total[:8] + 1e-06)


HOPS = (0, 1, 2, 1)
XY = [(dx, dy) for dx in range(4) for dy in range(4) if dx or dy]
XY.sort(key=lambda m: -HOPS[m[0]] - HOPS[m[1]])
RING4 = (2, 1, 3)
RING8 = (4, 3, 5, 2, 6, 1, 7)


def kernel(
    img_hbm,
    lab_hbm,
    one_hbm,
    two_hbm,
    slope_hbm,
    spatial_hbm,
    head_hbm,
    queue_hbm,
    cand_hbm,
    gen_hbm,
    off_hbm,
    loss_out,
    fresh_out,
    upd_out,
    lab,
    gen,
    off,
    slope,
    spatial,
    head,
    cand,
    img,
    w1,
    w2,
    w2t,
    qb,
    s1,
    s2,
    sd,
    sp,
    xt,
    ht,
    fac,
    spm,
    pooled,
    cm,
    c_rec,
    ch,
    x_rec,
    ch2,
    z_rec,
    half,
    pan,
    gb,
    r1,
    ta,
    tbf,
    tb,
    ra,
    uaf,
    ua,
    ubf,
    ub,
    ra2,
    zsf,
    zs,
    zr,
    ns,
    nr1,
    nr2,
    nr3,
    hgf,
    ld_sem,
    sem,
    rep_sem,
    core_sem,
    first_sem,
    second_sem,
):
    z_hi, x_me, core, z_lo, y_me = place()
    dp, rep = lax.axis_index("dp"), lax.axis_index("rep")
    z_me = z_hi * 2 + z_lo
    first_row = (dp * 8 + rep) * CHUNK

    def remote(src, dst, s, r, to):
        return pltpu.make_async_remote_copy(
            src_ref=src,
            dst_ref=dst,
            send_sem=s,
            recv_sem=r,
            device_id=to,
            device_id_type=MESH,
        )

    def wait_bytes(ref, sem):
        pltpu.make_async_copy(ref, ref, sem).wait()

    pairs = dict(
        cand=(cand_hbm, cand),
        gen=(gen_hbm, gen),
        img=(img_hbm, img),
        w1=(one_hbm, w1),
        slope=(slope_hbm, slope),
        w2=(two_hbm, w2),
        spatial=(spatial_hbm, spatial),
        head=(head_hbm, head),
        lab=(lab_hbm, lab),
        off=(off_hbm, off),
        queue=(queue_hbm, qb),
    )
    loads = {
        name: pltpu.make_async_copy(a, b, ld_sem.at[k])
        for k, (name, (a, b)) in enumerate(pairs.items())
    }
    loads["cand"].start()
    loads["gen"].start()

    barrier = pltpu.get_barrier_semaphore()
    friends = [dict(dx=a, dy=b) for a, b in XY]
    friends += [dict(dz=k) for k in RING8]
    friends += [dict(dlo=1, dy=k) for k in RING4] + [dict(dc=1)]
    for f in friends:
        pl.semaphore_signal(barrier, inc=1, device_id=peer(**f), device_id_type=MESH)

    loads["cand"].wait()
    loads["gen"].wait()
    mine = jnp.where(gen[0] == dp, 1.0, 0.0)
    cm[...] = (cand[...].astype(F32) * mine).astype(BF16)
    pl.semaphore_wait(barrier, len(friends))

    other_half = cm.at[pl.ds(pl.multiple_of((1 - core) * 32, 32), 32)]
    p_core = remote(other_half, c_rec, sem.at[0], sem.at[1], peer(dc=1))
    p_core.start()

    for name, cp in loads.items():
        if name not in ("cand", "gen"):
            cp.start()
    for buf in (s1, s2, sd, sp):
        for b in range(IMG):
            buf[b, 0:16, :] = jnp.zeros((16, 3 * C), BF16)
            buf[b, 240:TALL, :] = jnp.zeros((TALL - 240, 3 * C), BF16)
    pooled[...] = jnp.zeros((8, C), F32)
    uaf[...] = jnp.zeros((4, 48, 128), F32)
    ubf[...] = jnp.zeros((4, 48, 128), F32)
    zsf[...] = jnp.zeros((8, 48, 128), F32)

    quarter = lax.broadcasted_iota(jnp.int32, (2 * CELLS, C), 0) % PAD
    inside = quarter < SIDE

    def shifted(buf, b, v):
        before, after = pltpu.roll(v, 1, 0), pltpu.roll(v, 2 * CELLS - 1, 0)
        for k in range(2):
            part = slice(k * CELLS, (k + 1) * CELLS)
            buf[b + k, 16:240, 0:C] = before[part].astype(BF16)
            buf[b + k, 16:240, C : 2 * C] = v[part].astype(BF16)
            buf[b + k, 16:240, 2 * C : 3 * C] = after[part].astype(BF16)

    def flip(buf, b, v):
        for k in range(2):
            part = v[k * CELLS : (k + 1) * CELLS]
            tall = jnp.concatenate([part, jnp.zeros((32, C), F32)], axis=0)
            at = pl.ds(pl.multiple_of((b + k) * 256, 256), 256)
            buf[:, at] = tall.T.astype(BF16)

    loads["img"].wait()

    def prepare(i, _):
        b = 2 * i
        v = img[pl.ds(b, 2)].astype(F32)
        v = jnp.concatenate([v, jnp.zeros((2, SIDE, PAD - SIDE, C), F32)], axis=2)
        v = v.reshape(2 * CELLS, C)
        shifted(s1, b, v)
        flip(xt, b, v)
        return 0

    lax.fori_loop(0, IMG // 2, prepare, 0)

    p_core.wait_recv()
    own_half = cm[pl.ds(pl.multiple_of(core * 32, 32), 32)]
    ch[...] = (own_half.astype(F32) + c_rec[...].astype(F32)).astype(BF16)
    for k in RING4:
        remote(ch, x_rec.at[k - 1], sem.at[2], sem.at[3], peer(dx=k)).start()

    loads["w1"].wait()
    loads["slope"].wait()

    def conv(buf, w, b):
        out = None
        for r in range(3):
            rows = buf[pl.ds(b, 2), r * 16 : r * 16 + CELLS, :]
            term = dot(rows.reshape(2 * CELLS, 3 * C), w[r].reshape(3 * C, C))
            out = term if out is None else out + term
        return out

    def first(i, _):
        b = 2 * i
        pre = conv(s1, w1, b)
        f = jnp.where(inside, jnp.where(pre > 0, 1.0, slope[...]), 0.0)
        fac[pl.ds(b, 2)] = f.reshape(2, CELLS, C)
        h = pre * f
        shifted(s2, b, h)
        flip(ht, b, h)
        return 0

    lax.fori_loop(0, IMG // 2, first, 0)

    wait_bytes(x_rec, sem.at[3])
    whole = ch[...].astype(F32)
    for k in range(3):
        whole += x_rec[k].astype(F32)
    ch2[...] = whole.astype(BF16)
    for k in RING4:
        remote(ch2, z_rec.at[k - 1], sem.at[4], sem.at[5], peer(dz=2 * k)).start()

    loads["spatial"].wait()
    for p in range(SIDE):
        spm[1, p * PAD : p * PAD + SIDE, :] = spatial[p * SIDE : (p + 1) * SIDE, :]
        spm[1, p * PAD + SIDE : (p + 1) * PAD, :] = jnp.zeros((PAD - SIDE, C), F32)
    loads["w2"].wait()

    def second(i, _):
        b = 2 * i
        out = conv(s2, w2, b)
        for k in range(2):
            part = out[k * CELLS : (k + 1) * CELLS]
            part += s1[b + k, 16:240, C : 2 * C].astype(F32)
            pooled[pl.ds(b + k, 1), :] = jnp.sum(part * spm[1], axis=0, keepdims=True)
        return 0

    lax.fori_loop(0, IMG // 2, second, 0)

    wait_bytes(z_rec, sem.at[5])
    whole = ch2[...].astype(F32)
    for k in range(3):
        whole += z_rec[k].astype(F32)
    half[rep] = whole.astype(BF16)
    rep_moves = [(1, 2), (1, 1), (1, 3), (0, 2), (0, 1), (0, 3), (1, 0)]
    for k, (lo, dy) in enumerate(rep_moves):
        to = peer(dlo=lo, dy=dy)
        remote(half.at[rep], half.at[rep], sem.at[6], rep_sem.at[k], to).start()

    spm[0] = pltpu.roll(spm[1], 1, 0)
    spm[2] = pltpu.roll(spm[1], CELLS - 1, 0)
    for r in range(3):
        for s in range(3):
            turned = w2[2 - r, 2 - s].astype(F32).T
            w2t[r, s] = turned.astype(BF16)

    for name in ("head", "lab", "off", "queue"):
        loads[name].wait()
    po = pooled[...]
    embed = dot3(po, head[...])
    inv_len = lax.rsqrt(jnp.sum(embed * embed, axis=1, keepdims=True) + 1e-06)
    unit = embed * inv_len
    rows8 = lax.broadcasted_iota(jnp.int32, (8, 1), 0)
    labels = jnp.full((8, 1), -1, jnp.int32)
    for b in range(IMG):
        labels = jnp.where(rows8 == b, lab[b], labels)
    shift = off[0]

    def score(rows, slots, keep):
        scale = row_lengths(rows)
        hot = (labels == slots) & keep
        logits = 64.0 * (dot3(unit, rows, NT) * scale - jnp.where(hot, 0.4, 0.0))
        exps = jnp.where(keep, jnp.exp(logits), 0.0)
        total = jnp.sum(exps, axis=1, keepdims=True)
        at_label = jnp.sum(jnp.where(hot, logits, 0.0), axis=1, keepdims=True)
        pulls = jnp.concatenate([exps * scale, jnp.where(hot, scale, 0.0)], axis=0)
        return total, at_label, dot3(pulls, rows)

    total = jnp.zeros((8, 1), F32)
    at_label = jnp.zeros((8, 1), F32)
    pulled = jnp.zeros((16, E), F32)
    for k in range(4):
        rows = qb[k * 512 : (k + 1) * 512, :]
        slots = lax.broadcasted_iota(jnp.int32, (8, 512), 1) + k * 512
        fresh = ((slots - shift + QUEUE) & (QUEUE - 1)) < GEN
        t, a, u = score(rows, slots, jnp.logical_not(fresh))
        total, at_label, pulled = total + t, at_label + a, pulled + u

    my_rows = pl.ds(pl.multiple_of(core * 32, 32), 32)

    other_rows = pl.ds(pl.multiple_of((1 - core) * 32, 32), 32)

    def pass_on(which):
        dst = pan.at[which, my_rows]
        remote(half.at[which], dst, sem.at[7], sem.at[8], peer(dc=1)).start()

    pass_on(rep)
    for k in range(6, -1, -1):
        lo, dy = rep_moves[k]
        which = ((z_lo + lo) % 2) * 4 + (y_me - dy) % 4
        wait_bytes(half.at[which], rep_sem.at[k])
        pass_on(which)

    j = lax.broadcasted_iota(jnp.int32, (8, GEN // 2), 1)
    j = (j >> 5) * 64 + (j & 31) + shift
    rows = half[...].reshape(GEN // 2, E)
    t, a, u = score(rows, (j + core * 32) & (QUEUE - 1), j >= 0)
    total, at_label, pulled = total + t, at_label + a, pulled + u
    pan[:, my_rows, :] = half[...]
    wait_bytes(pan.at[:, other_rows], sem.at[8])
    rows = pan[:, other_rows, :].reshape(GEN // 2, E)
    t, a, u = score(rows, (j + (1 - core) * 32) & (QUEUE - 1), j >= 0)
    total, at_label, pulled = total + t, at_label + a, pulled + u
    loss = jnp.log(total) - at_label
    lanes = lax.broadcasted_iota(jnp.int32, (8, 128), 1)
    rows128 = lax.broadcasted_iota(jnp.int32, (8, 128), 0)
    loss_out[...] = jnp.sum(jnp.where(lanes == rows128, loss, 0.0), axis=0)[:IMG]
    d_unit = 64.0 * (pulled[0:8] / total - pulled[8:16])
    d_embed = (d_unit - unit * jnp.sum(d_unit * unit, axis=1, keepdims=True)) * inv_len
    d_embed = jnp.where(rows8 < IMG, d_embed, 0.0)
    d_pooled = dot3(d_embed, head[...], NT)

    for b in range(IMG):
        for s in range(3):
            sd[b, 16:240, s * C : (s + 1) * C] = (
                spm[s] * d_pooled[b : b + 1, :]
            ).astype(BF16)

    po_h = po.astype(BF16).astype(F32)
    de_h = d_embed.astype(BF16).astype(F32)
    left = jnp.concatenate([po_h, po_h, po - po_h, jnp.zeros_like(po)], axis=0)
    right = jnp.concatenate(
        [de_h, d_embed - de_h, de_h, jnp.zeros_like(d_embed)], axis=0
    )
    g_head = dot(left.T.astype(BF16), right.astype(BF16))
    zsf2 = hgf
    for k in range(2):
        for h in range(2):
            zsf2[pl.ds(k * 512 + h, 256, stride=2), :] = g_head[
                :, h * 256 + k * 128 : h * 256 + (k + 1) * 128
            ]
    for k in range(2):
        gb.reshape(ROWS, C)[2 * CONV_ROWS :, k * 128 : (k + 1) * 128] = zsf2[
            k * 512 : (k + 1) * 512, :
        ].astype(BF16)

    flat = gb.reshape(ROWS, C)

    def weight_grad(turned, buf, tap, base):
        r, s = 2 - tap // 3, 2 - tap % 3
        rows = buf[:, r * 16 : r * 16 + 256, s * C : (s + 1) * C].reshape(IMG * 256, C)
        flat[base + tap * 256 : base + (tap + 1) * 256, :] = dot(turned[...], rows).astype(
            BF16
        )

    def send(u, first, count):
        at = pl.ds(4 * u + first, count)
        src, dst = gb.at[at, 1 - core], r1.at[at]
        remote(src, dst, sem.at[9], core_sem.at[u], peer(dc=1)).start()

    def two(*taps):
        for tap in taps:
            weight_grad(ht, sd, tap, CONV_ROWS)

    def one(*taps):
        for tap in taps:
            weight_grad(xt, sp, tap, 0)

    def back(i, _):
        b = 2 * i
        out = conv(sd, w2t, b) * fac[pl.ds(b, 2)].reshape(2 * CELLS, C)
        shifted(sp, b, out)
        return 0

    def after_core(u, n):
        for unit in range(u, u + n):
            wait_bytes(r1.at[pl.ds(4 * unit, 4)], core_sem.at[unit])
            for x in range(4):
                a = 4 * unit + x
                v = gb[a, core].astype(F32) + r1[a].astype(F32)
                ta[unit, x] = v[:, 0:128].astype(BF16)
                for lo in range(2):
                    for y in range(4):
                        k, at = (lo * 4 + y) * CHUNK, (x * 2 + lo) * CHUNK
                        tbf[y, at : at + CHUNK, :] = v[k : k + CHUNK, 128:256]
            tb[unit] = tbf[...].astype(BF16)
        span, there, here = pl.ds(u, n), sem.at[10], first_sem.at[u]
        for k in RING4:
            src = ta.at[span, (x_me + k) % 4]
            remote(src, ra.at[k - 1, span], there, here, peer(dx=k)).start()
            src = tb.at[span, (y_me + k) % 4]
            remote(src, ra.at[k + 2, span], there, here, peer(dy=k)).start()

    def after_first(u, n):
        wait_bytes(ra.at[:, pl.ds(u, n)], first_sem.at[u])
        for unit in range(u, u + n):
            v = ta[unit, x_me].astype(F32)
            for k in range(3):
                v += ra[k, unit].astype(F32)
            for lo in range(2):
                for y in range(4):
                    k, at = (lo * 4 + y) * CHUNK, lo * CHUNK
                    uaf[y, at : at + CHUNK, :] = v[k : k + CHUNK]
            v = tb[unit, y_me].astype(F32)
            for k in range(3):
                v += ra[k + 3, unit].astype(F32)
            for x in range(4):
                ubf[x, 0:40, :] = v[x * 40 : (x + 1) * 40]
            ua[unit] = uaf[...].astype(BF16)
            ub[unit] = ubf[...].astype(BF16)
        span, there, here = pl.ds(u, n), sem.at[11], second_sem.at[u]
        for k in RING4:
            src = ua.at[span, (y_me + k) % 4]
            remote(src, ra2.at[k - 1, span], there, here, peer(dy=k)).start()
            src = ub.at[span, (x_me + k) % 4]
            remote(src, ra2.at[k + 2, span], there, here, peer(dx=k)).start()

    def after_second(u, n):
        wait_bytes(ra2.at[:, pl.ds(u, n)], second_sem.at[u])
        for unit in range(u, u + n):
            for side, own in enumerate((ua[unit, y_me], ub[unit, x_me])):
                v = own.astype(F32)
                for k in range(3):
                    v += ra2[3 * side + k, unit].astype(F32)
                for lo in range(2):
                    zsf[2 * unit + lo, side * CHUNK : (side + 1) * CHUNK, :] = v[
                        lo * CHUNK : (lo + 1) * CHUNK
                    ]

    def send_z(upper):
        for z in range(4 * upper, 4 * upper + 4):
            zs[z] = zsf[z].astype(BF16)
        for k in RING8:
            to = (z_me + k) % 8

            @pl.when(to // 4 == upper)
            def _():
                dst = zr.at[k - 1]
                remote(zs.at[to], dst, sem.at[12], sem.at[13], peer(dz=k)).start()

    def renew(k, _):
        at = pl.ds(pl.multiple_of(k * 256, 256), 256)
        slot = lax.broadcasted_iota(jnp.int32, (256, GEN), 0) + k * 256
        source = (slot - shift + QUEUE) & (QUEUE - 1)
        pick = jnp.where(
            source == lax.broadcasted_iota(jnp.int32, (256, GEN), 1), 1.0, 0.0
        ).astype(BF16)
        new = dot(pick, pan[...].reshape(GEN, E))
        old = qb[at, :].astype(F32)
        fresh_out[at, :] = jnp.where(source[:, 0:1] < GEN, new, old).astype(BF16)
        return 0

    two(6, 7, 8)
    send(3, 0, 4)
    two(1, 2, 3, 4, 5)
    send(2, 0, 4)
    two(0)
    lax.fori_loop(0, 2, back, 0)
    after_core(2, 2)
    lax.fori_loop(2, IMG // 2, back, 0)
    one(5, 6, 7, 8)
    send(1, 0, 4)
    one(0, 1, 2)
    send(0, 0, 2)
    one(3, 4)
    send(0, 2, 2)
    after_core(1, 1)
    after_core(0, 1)
    after_first(2, 2)
    lax.fori_loop(0, 4, renew, 0)
    after_first(1, 1)
    after_second(2, 2)
    send_z(1)
    after_first(0, 1)
    lax.fori_loop(4, 8, renew, 0)
    after_second(1, 1)
    after_second(0, 1)
    send_z(0)
    wait_bytes(zr, sem.at[13])
    v = zsf[z_me]
    for k in range(7):
        v += zr[k].astype(F32)
    low, high = v[0:CHUNK], v[CHUNK : 2 * CHUNK]

    row = first_row + lax.broadcasted_iota(jnp.int32, (CHUNK, 128), 0)
    in_one = row < CONV_ROWS
    in_head = row >= 2 * CONV_ROWS
    in_two = jnp.logical_not(in_one | in_head)
    sq = low * low + high * high
    for k, m in enumerate((in_one, in_two, in_head)):
        ns[0, k : k + 1, :] = jnp.sum(jnp.where(m, sq, 0.0), axis=0, keepdims=True)
    ns[0, 3:8, :] = jnp.zeros((5, 128), F32)

    def gather_sums(level, dst, moves):
        there, here = sem.at[14 + 2 * level], sem.at[15 + 2 * level]
        for k, m in enumerate(moves):
            remote(ns.at[level], dst.at[k], there, here, peer(**m)).start()
        wait_bytes(dst, here)
        s = ns[level]
        for k in range(len(moves)):
            s += dst[k]
        return s

    ns[1] = gather_sums(0, nr1, [dict(dx=a, dy=b) for a, b in XY])
    ns[2] = gather_sums(1, nr2, [dict(dz=k) for k in RING8])
    s = gather_sums(2, nr3, [dict(dc=1)])
    s = jnp.sum(s, axis=1, keepdims=True)
    scale = lax.rsqrt(s + 1e-06)
    conv_n, head_n = (9 * C * C) ** 0.5, (C * E) ** 0.5
    factor = jnp.where(
        in_one,
        scale[0:1] * conv_n,
        jnp.where(in_two, scale[1:2] * conv_n, scale[2:3] * head_n),
    )
    upd_out[pl.ds(0, CHUNK, stride=2), :] = low * factor
    upd_out[pl.ds(1, CHUNK, stride=2), :] = high * factor

    p_core.wait_send()
    sent = [
        (x_rec, 2),
        (z_rec, 4),
        (half.at[pl.ds(0, 7)], 6),
        (half, 7),
        (r1, 9),
        (ra, 10),
        (ra2, 11),
        (zr, 12),
        (nr1, 14),
        (nr2, 16),
        (nr3, 18),
    ]
    for ref, k in sent:
        wait_bytes(ref, sem.at[k])


SCRATCH = [
    pltpu.SMEM((IMG,), jnp.int32),
    pltpu.SMEM((32,), jnp.int32),
    pltpu.SMEM((1,), jnp.int32),
    VMEM((1, C), F32),
    VMEM((SIDE * SIDE, C), F32),
    VMEM((C, E), BF16),
    VMEM((64, E), BF16),
    VMEM((IMG, SIDE, SIDE, C), BF16),
    VMEM((3, 3, C, C), BF16),
    VMEM((3, 3, C, C), BF16),
    VMEM((3, 3, C, C), BF16),
    VMEM((QUEUE, E), BF16),
    VMEM((IMG, TALL, 3 * C), BF16),
    VMEM((IMG, TALL, 3 * C), BF16),
    VMEM((IMG, TALL, 3 * C), BF16),
    VMEM((IMG, TALL, 3 * C), BF16),
    VMEM((C, IMG * 256), BF16),
    VMEM((C, IMG * 256), BF16),
    VMEM((IMG, CELLS, C), F32),
    VMEM((3, CELLS, C), F32),
    VMEM((8, C), F32),
    VMEM((64, E), BF16),
    VMEM((32, E), BF16),
    VMEM((32, E), BF16),
    VMEM((3, 32, E), BF16),
    VMEM((32, E), BF16),
    VMEM((3, 32, E), BF16),
    VMEM((8, 32, E), BF16),
    VMEM((8, 64, E), BF16),
    VMEM((16, 2, 160, C), BF16),
    VMEM((16, 160, C), BF16),
    VMEM((4, 4, 160, 128), BF16),
    VMEM((4, 160, 128), F32),
    VMEM((4, 4, 160, 128), BF16),
    VMEM((6, 4, 160, 128), BF16),
    VMEM((4, 48, 128), F32),
    VMEM((4, 4, 48, 128), BF16),
    VMEM((4, 48, 128), F32),
    VMEM((4, 4, 48, 128), BF16),
    VMEM((6, 4, 48, 128), BF16),
    VMEM((8, 48, 128), F32),
    VMEM((8, 48, 128), BF16),
    VMEM((7, 48, 128), BF16),
    VMEM((3, 8, 128), F32),
    VMEM((15, 8, 128), F32),
    VMEM((7, 8, 128), F32),
    VMEM((1, 8, 128), F32),
    VMEM((1024, 128), F32),
    DMA((11,)),
    DMA((20,)),
    DMA((7,)),
    DMA((4,)),
    DMA((4,)),
    DMA((4,)),
]


def shards(
    images,
    labels,
    conv_one,
    conv_two,
    prelu_slope,
    spatial,
    head_weight,
    class_queue,
    candidates,
    generator,
    offset,
):
    far = pl.BlockSpec(memory_space=pl.ANY)
    near = pl.BlockSpec(memory_space=pltpu.VMEM)
    loss, fresh, update = pl.pallas_call(
        kernel,
        out_shape=(
            VMEM((IMG,), F32),
            VMEM((QUEUE, E), BF16),
            VMEM((2 * CHUNK, 128), F32),
        ),
        in_specs=[far] * 11,
        out_specs=(near, near, near),
        scratch_shapes=SCRATCH,
        name="whole_step",
        compiler_params=pltpu.CompilerParams(
            collective_id=0, has_side_effects=True, vmem_limit_bytes=56 << 20
        ),
    )(
        images,
        labels,
        conv_one,
        conv_two,
        prelu_slope.reshape(1, C),
        spatial,
        head_weight,
        class_queue,
        candidates,
        generator,
        offset,
    )
    return loss, fresh, update.reshape(2 * CHUNK * 128)


def solution(mesh):
    in_specs = (
        P(("dp", "rep"), None, None, None),
        P(("dp", "rep")),
        P(),
        P(),
        P(),
        P(),
        P(),
        P(),
        P(("dp", "rep"), None),
        P(),
        P(),
    )
    out_specs = (P(("dp", "rep")), P(), P(("dp", "rep")))
    return jax.shard_map(
        shards, mesh=mesh, in_specs=in_specs, out_specs=out_specs, check_vma=False
    )
```

```python
import functools

import jax
import jax.numpy as jnp
from jax import lax
from jax.experimental import pallas as pl
from jax.experimental.pallas import tpu as pltpu
from jax.sharding import PartitionSpec as P

F32 = jnp.float32
BF16 = jnp.bfloat16
MESH = pl.DeviceIdType.MESH
VMEM = pltpu.VMEM
DMA = pltpu.SemaphoreType.DMA

IMG, SIDE, C, E = 6, 14, 256, 512
PAD = 16
CELLS = SIDE * PAD
TALL = 288
QUEUE, GEN = 2048, 512
ROWS = 5120
CONV_ROWS = 2304
CHUNK = 20

NN = (((1,), (0,)), ((), ()))
NT = (((1,), (1,)), ((), ()))
TN = (((0,), (0,)), ((), ()))


def dot(a, b, dims=NN):
    return lax.dot_general(a, b, dims, preferred_element_type=F32)


def place():
    dp, rep = lax.axis_index("dp"), lax.axis_index("rep")
    return dp // 8, (dp // 2) % 4, dp % 2, rep // 4, rep % 4


def peer(dz=0, dx=0, dc=0, dy=0, dlo=0):
    z_hi, x, core, z_lo, y = place()
    z = (z_hi * 2 + (z_lo + dlo) % 2 + dz) % 8
    x, y, core = (x + dx) % 4, (y + dy) % 4, (core + dc) % 2
    return ((z // 2) * 4 + x) * 2 + core, (z % 2) * 4 + y


def stack3(v):
    high = v.astype(BF16).astype(F32)
    rest = v - high
    mid = rest.astype(BF16).astype(F32)
    low = rest - mid
    return jnp.concatenate([high, mid, low, jnp.zeros_like(v)], axis=0).astype(BF16)


def dot3(v, b, dims=NN):
    n = v.shape[0]
    out = dot(stack3(v), b, dims)
    return out[:n] + out[n : 2 * n] + out[2 * n : 3 * n]


def row_lengths(rows):
    f = rows.astype(F32)
    sq = f * f
    high = sq.astype(BF16)
    low = (sq - high.astype(F32)).astype(BF16)
    ones = jnp.ones((16, rows.shape[1]), BF16)
    total = dot(ones, high, NT) + dot(ones, low, NT)
    return lax.rsqrt(total[:8] + 1e-06)


HOPS = (0, 1, 2, 1)
XY = [(dx, dy) for dx in range(4) for dy in range(4) if dx or dy]
XY.sort(key=lambda m: -HOPS[m[0]] - HOPS[m[1]])
RING4 = (2, 1, 3)
RING8 = (4, 3, 5, 2, 6, 1, 7)


def kernel(
    img_hbm,
    lab_hbm,
    one_hbm,
    two_hbm,
    slope_hbm,
    spatial_hbm,
    head_hbm,
    queue_hbm,
    cand_hbm,
    gen_hbm,
    off_hbm,
    loss_out,
    fresh_out,
    upd_out,
    lab,
    gen,
    off,
    slope,
    spatial,
    head,
    cand,
    img,
    w1,
    w2,
    w2t,
    qb,
    s1,
    s2,
    sd,
    sp,
    xt,
    ht,
    fac,
    spm,
    spb,
    g2,
    pooled,
    cm,
    c_rec,
    ch,
    x_rec,
    ch2,
    z_rec,
    half,
    pan,
    gb,
    r1,
    ta,
    tbf,
    tb,
    ra,
    uaf,
    ua,
    ubf,
    ub,
    ra2,
    zsf,
    zs,
    zr,
    ns,
    nr1,
    nr2,
    nr3,
    hgf,
    ld_sem,
    sem,
    rep_sem,
    core_sem,
    first_sem,
    second_sem,
):
    z_hi, x_me, core, z_lo, y_me = place()
    dp, rep = lax.axis_index("dp"), lax.axis_index("rep")
    z_me = z_hi * 2 + z_lo
    first_row = (dp * 8 + rep) * CHUNK

    def remote(src, dst, s, r, to):
        return pltpu.make_async_remote_copy(
            src_ref=src,
            dst_ref=dst,
            send_sem=s,
            recv_sem=r,
            device_id=to,
            device_id_type=MESH,
        )

    def wait_bytes(ref, sem):
        pltpu.make_async_copy(ref, ref, sem).wait()

    pairs = dict(
        cand=(cand_hbm, cand),
        gen=(gen_hbm, gen),
        img=(img_hbm, img),
        w1=(one_hbm, w1),
        slope=(slope_hbm, slope),
        w2=(two_hbm, w2),
        spatial=(spatial_hbm, spatial),
        head=(head_hbm, head),
        lab=(lab_hbm, lab),
        off=(off_hbm, off),
        queue=(queue_hbm, qb),
    )
    loads = {
        name: pltpu.make_async_copy(a, b, ld_sem.at[k])
        for k, (name, (a, b)) in enumerate(pairs.items())
    }
    loads["cand"].start()
    loads["gen"].start()

    barrier = pltpu.get_barrier_semaphore()
    friends = [dict(dx=a, dy=b) for a, b in XY]
    friends += [dict(dz=k) for k in RING8]
    friends += [dict(dlo=1, dy=k) for k in RING4] + [dict(dc=1)]
    for f in friends:
        pl.semaphore_signal(barrier, inc=1, device_id=peer(**f), device_id_type=MESH)

    loads["cand"].wait()
    loads["gen"].wait()
    mine = jnp.where(gen[0] == dp, 1.0, 0.0)
    cm[...] = (cand[...].astype(F32) * mine).astype(BF16)
    pl.semaphore_wait(barrier, len(friends))

    other_half = cm.at[pl.ds(pl.multiple_of((1 - core) * 32, 32), 32)]
    p_core = remote(other_half, c_rec, sem.at[0], sem.at[1], peer(dc=1))
    p_core.start()

    for name, cp in loads.items():
        if name not in ("cand", "gen"):
            cp.start()
    for buf in (s1, s2, sd, sp):
        for b in range(IMG):
            buf[b, 0:16, :] = jnp.zeros((16, 3 * C), BF16)
            buf[b, 240:TALL, :] = jnp.zeros((TALL - 240, 3 * C), BF16)
    pooled[...] = jnp.zeros((8, C), F32)
    uaf[...] = jnp.zeros((4, 48, 128), F32)
    ubf[...] = jnp.zeros((4, 48, 128), F32)
    zsf[...] = jnp.zeros((8, 48, 128), F32)

    quarter = lax.broadcasted_iota(jnp.int32, (2 * CELLS, C), 0) % PAD
    inside = quarter < SIDE

    def shifted(buf, b, v):
        before, after = pltpu.roll(v, 1, 0), pltpu.roll(v, 2 * CELLS - 1, 0)
        for k in range(2):
            part = slice(k * CELLS, (k + 1) * CELLS)
            buf[b + k, 16:240, 0:C] = before[part].astype(BF16)
            buf[b + k, 16:240, C : 2 * C] = v[part].astype(BF16)
            buf[b + k, 16:240, 2 * C : 3 * C] = after[part].astype(BF16)

    def flip(buf, b, v):
        for k in range(2):
            part = v[k * CELLS : (k + 1) * CELLS]
            tall = jnp.concatenate([part, jnp.zeros((32, C), F32)], axis=0)
            at = pl.ds(pl.multiple_of((b + k) * 256, 256), 256)
            if buf is ht:
                buf[at, :] = tall.T.astype(BF16)
            else:
                buf[:, at] = tall.T.astype(BF16)

    loads["img"].wait()

    def prepare(i, _):
        b = 2 * i
        v = img[pl.ds(b, 2)].astype(F32)
        v = jnp.concatenate([v, jnp.zeros((2, SIDE, PAD - SIDE, C), F32)], axis=2)
        v = v.reshape(2 * CELLS, C)
        shifted(s1, b, v)
        flip(xt, b, v)
        return 0

    lax.fori_loop(0, IMG // 2, prepare, 0)

    p_core.wait_recv()
    own_half = cm[pl.ds(pl.multiple_of(core * 32, 32), 32)]
    ch[...] = (own_half.astype(F32) + c_rec[...].astype(F32)).astype(BF16)
    for k in RING4:
        remote(ch, x_rec.at[k - 1], sem.at[2], sem.at[3], peer(dx=k)).start()

    loads["w1"].wait()
    loads["slope"].wait()

    def conv(buf, w, b):
        out = None
        for r in range(3):
            rows = buf[pl.ds(b, 2), r * 16 : r * 16 + CELLS, :]
            term = dot(rows.reshape(2 * CELLS, 3 * C), w[r].reshape(3 * C, C))
            out = term if out is None else out + term
        return out

    def first(i, _):
        b = 2 * i
        pre = conv(s1, w1, b)
        f = jnp.where(inside, jnp.where(pre > 0, 1.0, slope[...]), 0.0)
        fac[pl.ds(b, 2)] = f.reshape(2, CELLS, C)
        h = pre * f
        shifted(s2, b, h)
        flip(ht, b, h)
        return 0

    lax.fori_loop(0, IMG // 2, first, 0)

    wait_bytes(x_rec, sem.at[3])
    whole = ch[...].astype(F32)
    for k in range(3):
        whole += x_rec[k].astype(F32)
    ch2[...] = whole.astype(BF16)
    for k in RING4:
        remote(ch2, z_rec.at[k - 1], sem.at[4], sem.at[5], peer(dz=2 * k)).start()

    loads["spatial"].wait()
    for p in range(SIDE):
        spm[1, p * PAD : p * PAD + SIDE, :] = spatial[p * SIDE : (p + 1) * SIDE, :]
        spm[1, p * PAD + SIDE : (p + 1) * PAD, :] = jnp.zeros((PAD - SIDE, C), F32)
    spm[0] = pltpu.roll(spm[1], 1, 0)
    spm[2] = pltpu.roll(spm[1], CELLS - 1, 0)
    spb[0:16, :] = jnp.zeros((16, 3 * C), BF16)
    spb[240:TALL, :] = jnp.zeros((TALL - 240, 3 * C), BF16)
    for k in range(3):
        spb[16:240, k * C : (k + 1) * C] = spm[k].astype(BF16)

    def unscaled(*taps):
        for tap in taps:
            r, c = 2 - tap // 3, 2 - tap % 3
            cells = spb[r * 16 : r * 16 + 256, c * C : (c + 1) * C]
            g2[tap] = dot(ht[...], cells).reshape(IMG, C, C)

    loads["w2"].wait()

    def second(i, _):
        b = 2 * i
        out = conv(s2, w2, b)
        for k in range(2):
            part = out[k * CELLS : (k + 1) * CELLS]
            part += s1[b + k, 16:240, C : 2 * C].astype(F32)
            pooled[pl.ds(b + k, 1), :] = jnp.sum(part * spm[1], axis=0, keepdims=True)
        return 0

    lax.fori_loop(0, IMG // 2, second, 0)
    unscaled(0, 1, 2, 3)

    wait_bytes(z_rec, sem.at[5])
    whole = ch2[...].astype(F32)
    for k in range(3):
        whole += z_rec[k].astype(F32)
    half[rep] = whole.astype(BF16)
    rep_moves = [(1, 2), (1, 1), (1, 3), (0, 2), (0, 1), (0, 3), (1, 0)]
    for k, (lo, dy) in enumerate(rep_moves):
        to = peer(dlo=lo, dy=dy)
        remote(half.at[rep], half.at[rep], sem.at[6], rep_sem.at[k], to).start()

    for r in range(3):
        for s in range(3):
            turned = w2[2 - r, 2 - s].astype(F32).T
            w2t[r, s] = turned.astype(BF16)

    for name in ("head", "lab", "off", "queue"):
        loads[name].wait()
    unscaled(4, 5, 6, 7, 8)
    po = pooled[...]
    embed = dot3(po, head[...])
    inv_len = lax.rsqrt(jnp.sum(embed * embed, axis=1, keepdims=True) + 1e-06)
    unit = embed * inv_len
    rows8 = lax.broadcasted_iota(jnp.int32, (8, 1), 0)
    labels = jnp.full((8, 1), -1, jnp.int32)
    for b in range(IMG):
        labels = jnp.where(rows8 == b, lab[b], labels)
    shift = off[0]

    def score(rows, slots, keep):
        scale = row_lengths(rows)
        hot = (labels == slots) & keep
        logits = 64.0 * (dot3(unit, rows, NT) * scale - jnp.where(hot, 0.4, 0.0))
        exps = jnp.where(keep, jnp.exp(logits), 0.0)
        total = jnp.sum(exps, axis=1, keepdims=True)
        at_label = jnp.sum(jnp.where(hot, logits, 0.0), axis=1, keepdims=True)
        pulls = jnp.concatenate([exps * scale, jnp.where(hot, scale, 0.0)], axis=0)
        return total, at_label, dot3(pulls, rows)

    total = jnp.zeros((8, 1), F32)
    at_label = jnp.zeros((8, 1), F32)
    pulled = jnp.zeros((16, E), F32)
    for k in range(4):
        rows = qb[k * 512 : (k + 1) * 512, :]
        slots = lax.broadcasted_iota(jnp.int32, (8, 512), 1) + k * 512
        fresh = ((slots - shift + QUEUE) & (QUEUE - 1)) < GEN
        t, a, u = score(rows, slots, jnp.logical_not(fresh))
        total, at_label, pulled = total + t, at_label + a, pulled + u

    my_rows = pl.ds(pl.multiple_of(core * 32, 32), 32)

    other_rows = pl.ds(pl.multiple_of((1 - core) * 32, 32), 32)

    def pass_on(which):
        dst = pan.at[which, my_rows]
        remote(half.at[which], dst, sem.at[7], sem.at[8], peer(dc=1)).start()

    pass_on(rep)
    for k in range(6, -1, -1):
        lo, dy = rep_moves[k]
        which = ((z_lo + lo) % 2) * 4 + (y_me - dy) % 4
        wait_bytes(half.at[which], rep_sem.at[k])
        pass_on(which)

    j = lax.broadcasted_iota(jnp.int32, (8, GEN // 2), 1)
    j = (j >> 5) * 64 + (j & 31) + shift
    rows = half[...].reshape(GEN // 2, E)
    t, a, u = score(rows, (j + core * 32) & (QUEUE - 1), j >= 0)
    total, at_label, pulled = total + t, at_label + a, pulled + u
    pan[:, my_rows, :] = half[...]
    wait_bytes(pan.at[:, other_rows], sem.at[8])
    rows = pan[:, other_rows, :].reshape(GEN // 2, E)
    t, a, u = score(rows, (j + (1 - core) * 32) & (QUEUE - 1), j >= 0)
    total, at_label, pulled = total + t, at_label + a, pulled + u
    loss = jnp.log(total) - at_label
    lanes = lax.broadcasted_iota(jnp.int32, (8, 128), 1)
    rows128 = lax.broadcasted_iota(jnp.int32, (8, 128), 0)
    loss_out[...] = jnp.sum(jnp.where(lanes == rows128, loss, 0.0), axis=0)[:IMG]
    d_unit = 64.0 * (pulled[0:8] / total - pulled[8:16])
    d_embed = (d_unit - unit * jnp.sum(d_unit * unit, axis=1, keepdims=True)) * inv_len
    d_embed = jnp.where(rows8 < IMG, d_embed, 0.0)
    d_pooled = dot3(d_embed, head[...], NT)

    po_h = po.astype(BF16).astype(F32)
    de_h = d_embed.astype(BF16).astype(F32)
    left = jnp.concatenate([po_h, po_h, po - po_h, jnp.zeros_like(po)], axis=0)
    right = jnp.concatenate(
        [de_h, d_embed - de_h, de_h, jnp.zeros_like(d_embed)], axis=0
    )
    g_head = dot(left.T.astype(BF16), right.astype(BF16))
    zsf2 = hgf
    for k in range(2):
        for h in range(2):
            zsf2[pl.ds(k * 512 + h, 256, stride=2), :] = g_head[
                :, h * 256 + k * 128 : h * 256 + (k + 1) * 128
            ]
    for k in range(2):
        gb.reshape(ROWS, C)[2 * CONV_ROWS :, k * 128 : (k + 1) * 128] = zsf2[
            k * 512 : (k + 1) * 512, :
        ].astype(BF16)

    flat = gb.reshape(ROWS, C)

    def weight_grad(turned, buf, tap, base):
        r, s = 2 - tap // 3, 2 - tap % 3
        rows = buf[:, r * 16 : r * 16 + 256, s * C : (s + 1) * C].reshape(IMG * 256, C)
        flat[base + tap * 256 : base + (tap + 1) * 256, :] = dot(turned[...], rows).astype(
            BF16
        )

    def send(u, first, count):
        at = pl.ds(4 * u + first, count)
        src, dst = gb.at[at, 1 - core], r1.at[at]
        remote(src, dst, sem.at[9], core_sem.at[u], peer(dc=1)).start()

    def two(*taps):
        for tap in taps:
            v = g2[tap, 0] * d_pooled[0:1, :]
            for b in range(1, IMG):
                v += g2[tap, b] * d_pooled[b : b + 1, :]
            at = CONV_ROWS + tap * 256
            flat[at : at + 256, :] = v.astype(BF16)

    def one(*taps):
        for tap in taps:
            weight_grad(xt, sp, tap, 0)

    def back(i, _):
        b = 2 * i
        out = conv(sd, w2t, b) * fac[pl.ds(b, 2)].reshape(2 * CELLS, C)
        shifted(sp, b, out)
        return 0

    def after_core(u, n):
        for unit in range(u, u + n):
            wait_bytes(r1.at[pl.ds(4 * unit, 4)], core_sem.at[unit])
            for x in range(4):
                a = 4 * unit + x
                v = gb[a, core].astype(F32) + r1[a].astype(F32)
                ta[unit, x] = v[:, 0:128].astype(BF16)
                for lo in range(2):
                    for y in range(4):
                        k, at = (lo * 4 + y) * CHUNK, (x * 2 + lo) * CHUNK
                        tbf[y, at : at + CHUNK, :] = v[k : k + CHUNK, 128:256]
            tb[unit] = tbf[...].astype(BF16)
        span, there, here = pl.ds(u, n), sem.at[10], first_sem.at[u]
        for k in RING4:
            src = ta.at[span, (x_me + k) % 4]
            remote(src, ra.at[k - 1, span], there, here, peer(dx=k)).start()
            src = tb.at[span, (y_me + k) % 4]
            remote(src, ra.at[k + 2, span], there, here, peer(dy=k)).start()

    def after_first(u, n):
        wait_bytes(ra.at[:, pl.ds(u, n)], first_sem.at[u])
        for unit in range(u, u + n):
            v = ta[unit, x_me].astype(F32)
            for k in range(3):
                v += ra[k, unit].astype(F32)
            for lo in range(2):
                for y in range(4):
                    k, at = (lo * 4 + y) * CHUNK, lo * CHUNK
                    uaf[y, at : at + CHUNK, :] = v[k : k + CHUNK]
            v = tb[unit, y_me].astype(F32)
            for k in range(3):
                v += ra[k + 3, unit].astype(F32)
            for x in range(4):
                ubf[x, 0:40, :] = v[x * 40 : (x + 1) * 40]
            ua[unit] = uaf[...].astype(BF16)
            ub[unit] = ubf[...].astype(BF16)
        span, there, here = pl.ds(u, n), sem.at[11], second_sem.at[u]
        for k in RING4:
            src = ua.at[span, (y_me + k) % 4]
            remote(src, ra2.at[k - 1, span], there, here, peer(dy=k)).start()
            src = ub.at[span, (x_me + k) % 4]
            remote(src, ra2.at[k + 2, span], there, here, peer(dx=k)).start()

    def after_second(u, n):
        wait_bytes(ra2.at[:, pl.ds(u, n)], second_sem.at[u])
        for unit in range(u, u + n):
            for side, own in enumerate((ua[unit, y_me], ub[unit, x_me])):
                v = own.astype(F32)
                for k in range(3):
                    v += ra2[3 * side + k, unit].astype(F32)
                for lo in range(2):
                    zsf[2 * unit + lo, side * CHUNK : (side + 1) * CHUNK, :] = v[
                        lo * CHUNK : (lo + 1) * CHUNK
                    ]

    def send_z(upper):
        for z in range(4 * upper, 4 * upper + 4):
            zs[z] = zsf[z].astype(BF16)
        for k in RING8:
            to = (z_me + k) % 8

            @pl.when(to // 4 == upper)
            def _():
                dst = zr.at[k - 1]
                remote(zs.at[to], dst, sem.at[12], sem.at[13], peer(dz=k)).start()

    def renew(k, _):
        at = pl.ds(pl.multiple_of(k * 256, 256), 256)
        slot = lax.broadcasted_iota(jnp.int32, (256, GEN), 0) + k * 256
        source = (slot - shift + QUEUE) & (QUEUE - 1)
        pick = jnp.where(
            source == lax.broadcasted_iota(jnp.int32, (256, GEN), 1), 1.0, 0.0
        ).astype(BF16)
        new = dot(pick, pan[...].reshape(GEN, E))
        old = qb[at, :].astype(F32)
        fresh_out[at, :] = jnp.where(source[:, 0:1] < GEN, new, old).astype(BF16)
        return 0

    two(6, 7, 8)
    send(3, 0, 4)
    two(1, 2, 3, 4, 5)
    send(2, 0, 4)
    two(0)
    for b in range(IMG):
        for s in range(3):
            sd[b, 16:240, s * C : (s + 1) * C] = (
                spm[s] * d_pooled[b : b + 1, :]
            ).astype(BF16)
    lax.fori_loop(0, 2, back, 0)
    after_core(2, 2)
    lax.fori_loop(2, IMG // 2, back, 0)
    one(5, 6, 7, 8)
    send(1, 0, 4)
    one(0, 1, 2)
    send(0, 0, 2)
    one(3)
    after_core(1, 1)
    one(4)
    send(0, 2, 2)
    after_core(0, 1)
    after_first(2, 2)
    after_first(1, 1)
    after_second(2, 2)
    send_z(1)
    after_first(0, 1)
    after_second(1, 1)
    after_second(0, 1)
    send_z(0)
    lax.fori_loop(0, 8, renew, 0)
    wait_bytes(zr, sem.at[13])
    v = zsf[z_me]
    for k in range(7):
        v += zr[k].astype(F32)
    low, high = v[0:CHUNK], v[CHUNK : 2 * CHUNK]

    row = first_row + lax.broadcasted_iota(jnp.int32, (CHUNK, 128), 0)
    in_one = row < CONV_ROWS
    in_head = row >= 2 * CONV_ROWS
    in_two = jnp.logical_not(in_one | in_head)
    sq = low * low + high * high
    for k, m in enumerate((in_one, in_two, in_head)):
        ns[0, k : k + 1, :] = jnp.sum(jnp.where(m, sq, 0.0), axis=0, keepdims=True)
    ns[0, 3:8, :] = jnp.zeros((5, 128), F32)

    def gather_sums(level, dst, moves):
        there, here = sem.at[14 + 2 * level], sem.at[15 + 2 * level]
        for k, m in enumerate(moves):
            remote(ns.at[level], dst.at[k], there, here, peer(**m)).start()
        wait_bytes(dst, here)
        s = ns[level]
        for k in range(len(moves)):
            s += dst[k]
        return s

    ns[1] = gather_sums(0, nr1, [dict(dx=a, dy=b) for a, b in XY])
    ns[2] = gather_sums(1, nr2, [dict(dz=k) for k in RING8])
    s = gather_sums(2, nr3, [dict(dc=1)])
    s = jnp.sum(s, axis=1, keepdims=True)
    scale = lax.rsqrt(s + 1e-06)
    conv_n, head_n = (9 * C * C) ** 0.5, (C * E) ** 0.5
    factor = jnp.where(
        in_one,
        scale[0:1] * conv_n,
        jnp.where(in_two, scale[1:2] * conv_n, scale[2:3] * head_n),
    )
    upd_out[pl.ds(0, CHUNK, stride=2), :] = low * factor
    upd_out[pl.ds(1, CHUNK, stride=2), :] = high * factor

    p_core.wait_send()
    sent = [
        (x_rec, 2),
        (z_rec, 4),
        (half.at[pl.ds(0, 7)], 6),
        (half, 7),
        (r1, 9),
        (ra, 10),
        (ra2, 11),
        (zr, 12),
        (nr1, 14),
        (nr2, 16),
        (nr3, 18),
    ]
    for ref, k in sent:
        wait_bytes(ref, sem.at[k])


SCRATCH = [
    pltpu.SMEM((IMG,), jnp.int32),
    pltpu.SMEM((32,), jnp.int32),
    pltpu.SMEM((1,), jnp.int32),
    VMEM((1, C), F32),
    VMEM((SIDE * SIDE, C), F32),
    VMEM((C, E), BF16),
    VMEM((64, E), BF16),
    VMEM((IMG, SIDE, SIDE, C), BF16),
    VMEM((3, 3, C, C), BF16),
    VMEM((3, 3, C, C), BF16),
    VMEM((3, 3, C, C), BF16),
    VMEM((QUEUE, E), BF16),
    VMEM((IMG, TALL, 3 * C), BF16),
    VMEM((IMG, TALL, 3 * C), BF16),
    VMEM((IMG, TALL, 3 * C), BF16),
    VMEM((IMG, TALL, 3 * C), BF16),
    VMEM((C, IMG * 256), BF16),
    VMEM((IMG * 256, 256), BF16),
    VMEM((IMG, CELLS, C), F32),
    VMEM((3, CELLS, C), F32),
    VMEM((TALL, 3 * C), BF16),
    VMEM((9, IMG, C, C), F32),
    VMEM((8, C), F32),
    VMEM((64, E), BF16),
    VMEM((32, E), BF16),
    VMEM((32, E), BF16),
    VMEM((3, 32, E), BF16),
    VMEM((32, E), BF16),
    VMEM((3, 32, E), BF16),
    VMEM((8, 32, E), BF16),
    VMEM((8, 64, E), BF16),
    VMEM((16, 2, 160, C), BF16),
    VMEM((16, 160, C), BF16),
    VMEM((4, 4, 160, 128), BF16),
    VMEM((4, 160, 128), F32),
    VMEM((4, 4, 160, 128), BF16),
    VMEM((6, 4, 160, 128), BF16),
    VMEM((4, 48, 128), F32),
    VMEM((4, 4, 48, 128), BF16),
    VMEM((4, 48, 128), F32),
    VMEM((4, 4, 48, 128), BF16),
    VMEM((6, 4, 48, 128), BF16),
    VMEM((8, 48, 128), F32),
    VMEM((8, 48, 128), BF16),
    VMEM((7, 48, 128), BF16),
    VMEM((3, 8, 128), F32),
    VMEM((15, 8, 128), F32),
    VMEM((7, 8, 128), F32),
    VMEM((1, 8, 128), F32),
    VMEM((1024, 128), F32),
    DMA((11,)),
    DMA((20,)),
    DMA((7,)),
    DMA((4,)),
    DMA((4,)),
    DMA((4,)),
]


def shards(
    images,
    labels,
    conv_one,
    conv_two,
    prelu_slope,
    spatial,
    head_weight,
    class_queue,
    candidates,
    generator,
    offset,
):
    far = pl.BlockSpec(memory_space=pl.ANY)
    near = pl.BlockSpec(memory_space=pltpu.VMEM)
    loss, fresh, update = pl.pallas_call(
        kernel,
        out_shape=(
            VMEM((IMG,), F32),
            VMEM((QUEUE, E), BF16),
            VMEM((2 * CHUNK, 128), F32),
        ),
        in_specs=[far] * 11,
        out_specs=(near, near, near),
        scratch_shapes=SCRATCH,
        name="whole_step",
        compiler_params=pltpu.CompilerParams(
            collective_id=0, has_side_effects=True, vmem_limit_bytes=56 << 20
        ),
    )(
        images,
        labels,
        conv_one,
        conv_two,
        prelu_slope.reshape(1, C),
        spatial,
        head_weight,
        class_queue,
        candidates,
        generator,
        offset,
    )
    return loss, fresh, update.reshape(2 * CHUNK * 128)


def solution(mesh):
    in_specs = (
        P(("dp", "rep"), None, None, None),
        P(("dp", "rep")),
        P(),
        P(),
        P(),
        P(),
        P(),
        P(),
        P(("dp", "rep"), None),
        P(),
        P(),
    )
    out_specs = (P(("dp", "rep")), P(), P(("dp", "rep")))
    return jax.shard_map(
        shards, mesh=mesh, in_specs=in_specs, out_specs=out_specs, check_vma=False
    )
```

```python
import functools

import jax
import jax.numpy as jnp
from jax import lax
from jax.experimental import pallas as pl
from jax.experimental.pallas import tpu as pltpu
from jax.sharding import PartitionSpec as P

F32 = jnp.float32
BF16 = jnp.bfloat16
MESH = pl.DeviceIdType.MESH
VMEM = pltpu.VMEM
DMA = pltpu.SemaphoreType.DMA

IMG, SIDE, C, E = 6, 14, 256, 512
PAD = 16
CELLS = SIDE * PAD
TALL = 288
QUEUE, GEN = 2048, 512
ROWS = 5120
CONV_ROWS = 2304
CHUNK = 20

NN = (((1,), (0,)), ((), ()))
NT = (((1,), (1,)), ((), ()))
TN = (((0,), (0,)), ((), ()))


def dot(a, b, dims=NN):
    return lax.dot_general(a, b, dims, preferred_element_type=F32)


def place():
    dp, rep = lax.axis_index("dp"), lax.axis_index("rep")
    return dp // 8, (dp // 2) % 4, dp % 2, rep // 4, rep % 4


def peer(dz=0, dx=0, dc=0, dy=0, dlo=0):
    z_hi, x, core, z_lo, y = place()
    z = (z_hi * 2 + (z_lo + dlo) % 2 + dz) % 8
    x, y, core = (x + dx) % 4, (y + dy) % 4, (core + dc) % 2
    return ((z // 2) * 4 + x) * 2 + core, (z % 2) * 4 + y


def stack3(v):
    high = v.astype(BF16).astype(F32)
    rest = v - high
    mid = rest.astype(BF16).astype(F32)
    low = rest - mid
    return jnp.concatenate([high, mid, low, jnp.zeros_like(v)], axis=0).astype(BF16)


def dot3(v, b, dims=NN):
    n = v.shape[0]
    out = dot(stack3(v), b, dims)
    return out[:n] + out[n : 2 * n] + out[2 * n : 3 * n]


def row_lengths(rows):
    f = rows.astype(F32)
    sq = f * f
    high = sq.astype(BF16)
    low = (sq - high.astype(F32)).astype(BF16)
    ones = jnp.ones((16, rows.shape[1]), BF16)
    total = dot(ones, high, NT) + dot(ones, low, NT)
    return lax.rsqrt(total[:8] + 1e-06)


HOPS = (0, 1, 2, 1)
XY = [(dx, dy) for dx in range(4) for dy in range(4) if dx or dy]
XY.sort(key=lambda m: -HOPS[m[0]] - HOPS[m[1]])
RING4 = (2, 1, 3)
RING8 = (4, 3, 5, 2, 6, 1, 7)


def kernel(
    img_hbm,
    lab_hbm,
    one_hbm,
    two_hbm,
    slope_hbm,
    spatial_hbm,
    head_hbm,
    queue_hbm,
    cand_hbm,
    gen_hbm,
    off_hbm,
    loss_out,
    fresh_out,
    upd_out,
    lab,
    gen,
    off,
    slope,
    spatial,
    head,
    cand,
    img,
    w1,
    w2,
    w2t,
    qb,
    s1,
    s2,
    sd,
    sp,
    xt,
    ht,
    fac,
    spm,
    pooled,
    cm,
    c_rec,
    ch,
    x_rec,
    ch2,
    z_rec,
    half,
    pan,
    gb,
    r1,
    ta,
    tbf,
    tb,
    ra,
    uaf,
    ua,
    ubf,
    ub,
    ra2,
    zsf,
    zs,
    zr,
    ns,
    nr1,
    nr2,
    nr3,
    hgf,
    ld_sem,
    sem,
    rep_sem,
    core_sem,
    first_sem,
    second_sem,
):
    z_hi, x_me, core, z_lo, y_me = place()
    dp, rep = lax.axis_index("dp"), lax.axis_index("rep")
    z_me = z_hi * 2 + z_lo
    first_row = (dp * 8 + rep) * CHUNK

    def remote(src, dst, s, r, to):
        return pltpu.make_async_remote_copy(
            src_ref=src,
            dst_ref=dst,
            send_sem=s,
            recv_sem=r,
            device_id=to,
            device_id_type=MESH,
        )

    def wait_bytes(ref, sem):
        pltpu.make_async_copy(ref, ref, sem).wait()

    pairs = dict(
        cand=(cand_hbm, cand),
        gen=(gen_hbm, gen),
        img=(img_hbm, img),
        w1=(one_hbm, w1),
        slope=(slope_hbm, slope),
        w2=(two_hbm, w2),
        spatial=(spatial_hbm, spatial),
        head=(head_hbm, head),
        lab=(lab_hbm, lab),
        off=(off_hbm, off),
        queue=(queue_hbm, qb),
    )
    loads = {
        name: pltpu.make_async_copy(a, b, ld_sem.at[k])
        for k, (name, (a, b)) in enumerate(pairs.items())
    }
    loads["cand"].start()
    loads["gen"].start()

    barrier = pltpu.get_barrier_semaphore()
    friends = [dict(dx=a, dy=b) for a, b in XY]
    friends += [dict(dz=k) for k in RING8]
    friends += [dict(dlo=1, dy=k) for k in RING4] + [dict(dc=1)]
    for f in friends:
        pl.semaphore_signal(barrier, inc=1, device_id=peer(**f), device_id_type=MESH)

    loads["cand"].wait()
    loads["gen"].wait()
    mine = jnp.where(gen[0] == dp, 1.0, 0.0)
    cm[...] = (cand[...].astype(F32) * mine).astype(BF16)
    pl.semaphore_wait(barrier, len(friends))

    other_half = cm.at[pl.ds(pl.multiple_of((1 - core) * 32, 32), 32)]
    p_core = remote(other_half, c_rec, sem.at[0], sem.at[1], peer(dc=1))
    p_core.start()

    for name, cp in loads.items():
        if name not in ("cand", "gen"):
            cp.start()
    for buf in (s1, s2, sd, sp):
        for b in range(IMG):
            buf[b, 0:16, :] = jnp.zeros((16, 3 * C), BF16)
            buf[b, 240:TALL, :] = jnp.zeros((TALL - 240, 3 * C), BF16)
    pooled[...] = jnp.zeros((16, C), F32)
    uaf[...] = jnp.zeros((4, 48, 128), F32)
    ubf[...] = jnp.zeros((4, 48, 128), F32)
    zsf[...] = jnp.zeros((8, 48, 128), F32)

    quarter = lax.broadcasted_iota(jnp.int32, (2 * CELLS, C), 0) % PAD
    inside = quarter < SIDE

    def shifted(buf, b, v):
        before, after = pltpu.roll(v, 1, 0), pltpu.roll(v, 2 * CELLS - 1, 0)
        for k in range(2):
            part = slice(k * CELLS, (k + 1) * CELLS)
            buf[b + k, 16:240, 0:C] = before[part].astype(BF16)
            buf[b + k, 16:240, C : 2 * C] = v[part].astype(BF16)
            buf[b + k, 16:240, 2 * C : 3 * C] = after[part].astype(BF16)

    def flip(buf, b, v):
        for k in range(2):
            part = v[k * CELLS : (k + 1) * CELLS]
            tall = jnp.concatenate([part, jnp.zeros((32, C), F32)], axis=0)
            at = pl.ds(pl.multiple_of((b + k) * 256, 256), 256)
            buf[:, at] = tall.T.astype(BF16)

    loads["img"].wait()

    def prepare(i, _):
        b = 2 * i
        v = img[pl.ds(b, 2)].astype(F32)
        v = jnp.concatenate([v, jnp.zeros((2, SIDE, PAD - SIDE, C), F32)], axis=2)
        v = v.reshape(2 * CELLS, C)
        shifted(s1, b, v)
        flip(xt, b, v)
        return 0

    lax.fori_loop(0, IMG // 2, prepare, 0)

    p_core.wait_recv()
    own_half = cm[pl.ds(pl.multiple_of(core * 32, 32), 32)]
    ch[...] = (own_half.astype(F32) + c_rec[...].astype(F32)).astype(BF16)
    for k in RING4:
        remote(ch, x_rec.at[k - 1], sem.at[2], sem.at[3], peer(dx=k)).start()

    loads["w1"].wait()
    loads["slope"].wait()

    def conv(buf, w, b):
        out = None
        for r in range(3):
            rows = buf[pl.ds(b, 2), r * 16 : r * 16 + CELLS, :]
            term = dot(rows.reshape(2 * CELLS, 3 * C), w[r].reshape(3 * C, C))
            out = term if out is None else out + term
        return out

    def first(i, _):
        b = 2 * i
        pre = conv(s1, w1, b)
        f = jnp.where(inside, jnp.where(pre > 0, 1.0, slope[...]), 0.0)
        fac[pl.ds(b, 2)] = f.reshape(2, CELLS, C)
        h = pre * f
        shifted(s2, b, h)
        flip(ht, b, h)
        return 0

    lax.fori_loop(0, IMG // 2, first, 0)

    wait_bytes(x_rec, sem.at[3])
    whole = ch[...].astype(F32)
    for k in range(3):
        whole += x_rec[k].astype(F32)
    ch2[...] = whole.astype(BF16)
    for k in RING4:
        remote(ch2, z_rec.at[k - 1], sem.at[4], sem.at[5], peer(dz=2 * k)).start()

    loads["spatial"].wait()
    for p in range(SIDE):
        spm[1, p * PAD : p * PAD + SIDE, :] = spatial[p * SIDE : (p + 1) * SIDE, :]
        spm[1, p * PAD + SIDE : (p + 1) * PAD, :] = jnp.zeros((PAD - SIDE, C), F32)
    loads["w2"].wait()

    def second(i, _):
        b = 2 * i
        out = conv(s2, w2, b)
        for k in range(2):
            part = out[k * CELLS : (k + 1) * CELLS]
            part += s1[b + k, 16:240, C : 2 * C].astype(F32)
            pooled[pl.ds(b + k, 1), :] = jnp.sum(part * spm[1], axis=0, keepdims=True)
        return 0

    lax.fori_loop(0, IMG // 2, second, 0)

    wait_bytes(z_rec, sem.at[5])
    whole = ch2[...].astype(F32)
    for k in range(3):
        whole += z_rec[k].astype(F32)
    half[rep] = whole.astype(BF16)
    rep_moves = [(1, 2), (1, 1), (1, 3), (0, 2), (0, 1), (0, 3), (1, 0)]
    for k, (lo, dy) in enumerate(rep_moves):
        to = peer(dlo=lo, dy=dy)
        remote(half.at[rep], half.at[rep], sem.at[6], rep_sem.at[k], to).start()

    spm[0] = pltpu.roll(spm[1], 1, 0)
    spm[2] = pltpu.roll(spm[1], CELLS - 1, 0)
    for r in range(3):
        for s in range(3):
            turned = w2[2 - r, 2 - s].astype(F32).T
            w2t[r, s] = turned.astype(BF16)

    for name in ("head", "lab", "off", "queue"):
        loads[name].wait()
    po = pooled[0:8, :]
    embed = dot3(po, head[...])
    inv_len = lax.rsqrt(jnp.sum(embed * embed, axis=1, keepdims=True) + 1e-06)
    unit = embed * inv_len
    rows8 = lax.broadcasted_iota(jnp.int32, (8, 1), 0)
    labels = jnp.full((8, 1), -1, jnp.int32)
    for b in range(IMG):
        labels = jnp.where(rows8 == b, lab[b], labels)
    shift = off[0]

    def score(rows, slots, keep):
        scale = row_lengths(rows)
        hot = (labels == slots) & keep
        logits = 64.0 * (dot3(unit, rows, NT) * scale - jnp.where(hot, 0.4, 0.0))
        exps = jnp.where(keep, jnp.exp(logits), 0.0)
        total = jnp.sum(exps, axis=1, keepdims=True)
        at_label = jnp.sum(jnp.where(hot, logits, 0.0), axis=1, keepdims=True)
        pulls = jnp.concatenate([exps * scale, jnp.where(hot, scale, 0.0)], axis=0)
        return total, at_label, dot3(pulls, rows)

    total = jnp.zeros((8, 1), F32)
    at_label = jnp.zeros((8, 1), F32)
    pulled = jnp.zeros((16, E), F32)
    for k in range(4):
        rows = qb[k * 512 : (k + 1) * 512, :]
        slots = lax.broadcasted_iota(jnp.int32, (8, 512), 1) + k * 512
        fresh = ((slots - shift + QUEUE) & (QUEUE - 1)) < GEN
        t, a, u = score(rows, slots, jnp.logical_not(fresh))
        total, at_label, pulled = total + t, at_label + a, pulled + u

    my_rows = pl.ds(pl.multiple_of(core * 32, 32), 32)

    other_rows = pl.ds(pl.multiple_of((1 - core) * 32, 32), 32)

    def pass_on(which):
        dst = pan.at[which, my_rows]
        remote(half.at[which], dst, sem.at[7], sem.at[8], peer(dc=1)).start()

    pass_on(rep)
    for k in range(6, -1, -1):
        lo, dy = rep_moves[k]
        which = ((z_lo + lo) % 2) * 4 + (y_me - dy) % 4
        wait_bytes(half.at[which], rep_sem.at[k])
        pass_on(which)

    j = lax.broadcasted_iota(jnp.int32, (8, GEN // 2), 1)
    j = (j >> 5) * 64 + (j & 31) + shift
    rows = half[...].reshape(GEN // 2, E)
    t, a, u = score(rows, (j + core * 32) & (QUEUE - 1), j >= 0)
    total, at_label, pulled = total + t, at_label + a, pulled + u
    pan[:, my_rows, :] = half[...]
    wait_bytes(pan.at[:, other_rows], sem.at[8])
    rows = pan[:, other_rows, :].reshape(GEN // 2, E)
    t, a, u = score(rows, (j + (1 - core) * 32) & (QUEUE - 1), j >= 0)
    total, at_label, pulled = total + t, at_label + a, pulled + u
    loss = jnp.log(total) - at_label
    lanes = lax.broadcasted_iota(jnp.int32, (8, 128), 1)
    rows128 = lax.broadcasted_iota(jnp.int32, (8, 128), 0)
    loss_out[...] = jnp.sum(jnp.where(lanes == rows128, loss, 0.0), axis=0)[:IMG]
    d_unit = 64.0 * (pulled[0:8] / total - pulled[8:16])
    d_embed = (d_unit - unit * jnp.sum(d_unit * unit, axis=1, keepdims=True)) * inv_len
    d_embed = jnp.where(rows8 < IMG, d_embed, 0.0)
    d_pooled = dot3(d_embed, head[...], NT)

    for b in range(IMG):
        for s in range(3):
            sd[b, 16:240, s * C : (s + 1) * C] = (
                spm[s] * d_pooled[b : b + 1, :]
            ).astype(BF16)

    po_h = po.astype(BF16).astype(F32)
    de_h = d_embed.astype(BF16).astype(F32)
    left = jnp.concatenate([po_h, po_h, po - po_h, jnp.zeros_like(po)], axis=0)
    right = jnp.concatenate(
        [de_h, d_embed - de_h, de_h, jnp.zeros_like(d_embed)], axis=0
    )
    g_head = dot(left.T.astype(BF16), right.astype(BF16))
    zsf2 = hgf
    for k in range(2):
        for h in range(2):
            zsf2[pl.ds(k * 512 + h, 256, stride=2), :] = g_head[
                :, h * 256 + k * 128 : h * 256 + (k + 1) * 128
            ]
    for k in range(2):
        gb.reshape(ROWS, C)[2 * CONV_ROWS :, k * 128 : (k + 1) * 128] = zsf2[
            k * 512 : (k + 1) * 512, :
        ].astype(BF16)

    flat = gb.reshape(ROWS, C)

    def weight_grad(turned, buf, tap, base):
        r, s = 2 - tap // 3, 2 - tap % 3
        rows = buf[:, r * 16 : r * 16 + 256, s * C : (s + 1) * C].reshape(IMG * 256, C)
        flat[base + tap * 256 : base + (tap + 1) * 256, :] = dot(turned[...], rows).astype(
            BF16
        )

    def send(u, first, count):
        at = pl.ds(4 * u + first, count)
        src, dst = gb.at[at, 1 - core], r1.at[at]
        remote(src, dst, sem.at[9], core_sem.at[u], peer(dc=1)).start()

    def two(*taps):
        for tap in taps:
            weight_grad(ht, sd, tap, CONV_ROWS)

    def one(*taps):
        for tap in taps:
            weight_grad(xt, sp, tap, 0)

    def back(i, _):
        b = 2 * i
        out = conv(sd, w2t, b) * fac[pl.ds(b, 2)].reshape(2 * CELLS, C)
        shifted(sp, b, out)
        return 0

    def after_core(u, n):
        for unit in range(u, u + n):
            wait_bytes(r1.at[pl.ds(4 * unit, 4)], core_sem.at[unit])
            for x in range(4):
                a = 4 * unit + x
                v = gb[a, core].astype(F32) + r1[a].astype(F32)
                ta[unit, x] = v[:, 0:128].astype(BF16)
                for lo in range(2):
                    for y in range(4):
                        k, at = (lo * 4 + y) * CHUNK, (x * 2 + lo) * CHUNK
                        tbf[y, at : at + CHUNK, :] = v[k : k + CHUNK, 128:256]
            tb[unit] = tbf[:, 0:160, :].astype(BF16)
        span, there, here = pl.ds(u, n), sem.at[10], first_sem.at[u]
        for k in RING4:
            src = ta.at[span, (x_me + k) % 4]
            remote(src, ra.at[k - 1, span], there, here, peer(dx=k)).start()
            src = tb.at[span, (y_me + k) % 4]
            remote(src, ra.at[k + 2, span], there, here, peer(dy=k)).start()

    def after_first(u, n):
        wait_bytes(ra.at[:, pl.ds(u, n)], first_sem.at[u])
        for unit in range(u, u + n):
            v = ta[unit, x_me].astype(F32)
            for k in range(3):
                v += ra[k, unit].astype(F32)
            for lo in range(2):
                for y in range(4):
                    k, at = (lo * 4 + y) * CHUNK, lo * CHUNK
                    uaf[y, at : at + CHUNK, :] = v[k : k + CHUNK]
            v = tb[unit, y_me].astype(F32)
            for k in range(3):
                v += ra[k + 3, unit].astype(F32)
            for x in range(4):
                ubf[x, 0:40, :] = v[x * 40 : (x + 1) * 40]
            ua[unit] = uaf[...].astype(BF16)
            ub[unit] = ubf[...].astype(BF16)
        span, there, here = pl.ds(u, n), sem.at[11], second_sem.at[u]
        for k in RING4:
            src = ua.at[span, (y_me + k) % 4]
            remote(src, ra2.at[k - 1, span], there, here, peer(dy=k)).start()
            src = ub.at[span, (x_me + k) % 4]
            remote(src, ra2.at[k + 2, span], there, here, peer(dx=k)).start()

    def after_second(u, n):
        wait_bytes(ra2.at[:, pl.ds(u, n)], second_sem.at[u])
        for unit in range(u, u + n):
            for side, own in enumerate((ua[unit, y_me], ub[unit, x_me])):
                v = own.astype(F32)
                for k in range(3):
                    v += ra2[3 * side + k, unit].astype(F32)
                for lo in range(2):
                    zsf[2 * unit + lo, side * CHUNK : (side + 1) * CHUNK, :] = v[
                        lo * CHUNK : (lo + 1) * CHUNK
                    ]

    def send_z(upper):
        for z in range(4 * upper, 4 * upper + 4):
            zs[z] = zsf[z].astype(BF16)
        for k in RING8:
            to = (z_me + k) % 8

            @pl.when(to // 4 == upper)
            def _():
                dst = zr.at[k - 1]
                remote(zs.at[to], dst, sem.at[12], sem.at[13], peer(dz=k)).start()

    def renew(k, _):
        at = pl.ds(pl.multiple_of(k * 256, 256), 256)
        slot = lax.broadcasted_iota(jnp.int32, (256, GEN), 0) + k * 256
        source = (slot - shift + QUEUE) & (QUEUE - 1)
        pick = jnp.where(
            source == lax.broadcasted_iota(jnp.int32, (256, GEN), 1), 1.0, 0.0
        ).astype(BF16)
        new = dot(pick, pan[...].reshape(GEN, E))
        old = qb[at, :].astype(F32)
        fresh_out[at, :] = jnp.where(source[:, 0:1] < GEN, new, old).astype(BF16)
        return 0

    two(6, 7, 8)
    send(3, 0, 4)
    two(1, 2, 3, 4, 5)
    send(2, 0, 4)
    two(0)
    lax.fori_loop(0, 2, back, 0)
    after_core(2, 2)
    lax.fori_loop(2, IMG // 2, back, 0)
    one(5, 6, 7, 8)
    send(1, 0, 4)
    one(0, 1, 2)
    send(0, 0, 2)
    one(3, 4)
    send(0, 2, 2)
    after_core(1, 1)
    after_core(0, 1)
    after_first(2, 2)
    lax.fori_loop(0, 4, renew, 0)
    after_first(1, 1)
    after_second(2, 2)
    send_z(1)
    after_first(0, 1)
    lax.fori_loop(4, 8, renew, 0)
    after_second(1, 1)
    after_second(0, 1)
    send_z(0)
    wait_bytes(zr, sem.at[13])
    v = zsf[z_me]
    for k in range(7):
        v += zr[k].astype(F32)
    low, high = v[0:CHUNK], v[CHUNK : 2 * CHUNK]

    row = first_row + lax.broadcasted_iota(jnp.int32, (CHUNK, 128), 0)
    in_one = row < CONV_ROWS
    in_head = row >= 2 * CONV_ROWS
    in_two = jnp.logical_not(in_one | in_head)
    sq = low * low + high * high
    for k, m in enumerate((in_one, in_two, in_head)):
        ns[0, k : k + 1, :] = jnp.sum(jnp.where(m, sq, 0.0), axis=0, keepdims=True)
    ns[0, 3:8, :] = jnp.zeros((5, 128), F32)

    def gather_sums(level, dst, moves):
        there, here = sem.at[14 + 2 * level], sem.at[15 + 2 * level]
        for k, m in enumerate(moves):
            remote(ns.at[level], dst.at[k], there, here, peer(**m)).start()
        wait_bytes(dst, here)
        s = ns[level]
        for k in range(len(moves)):
            s += dst[k]
        return s

    ns[1] = gather_sums(0, nr1, [dict(dx=a, dy=b) for a, b in XY])
    ns[2] = gather_sums(1, nr2, [dict(dz=k) for k in RING8])
    s = gather_sums(2, nr3, [dict(dc=1)])
    s = jnp.sum(s, axis=1, keepdims=True)
    scale = lax.rsqrt(s + 1e-06)
    conv_n, head_n = (9 * C * C) ** 0.5, (C * E) ** 0.5
    factor = jnp.where(
        in_one,
        scale[0:1] * conv_n,
        jnp.where(in_two, scale[1:2] * conv_n, scale[2:3] * head_n),
    )
    hgf[pl.ds(0, CHUNK, stride=2), :] = low * factor
    hgf[pl.ds(1, CHUNK, stride=2), :] = high * factor
    upd_out[...] = hgf[0 : 2 * CHUNK, :]

    p_core.wait_send()
    sent = [
        (x_rec, 2),
        (z_rec, 4),
        (half.at[pl.ds(0, 7)], 6),
        (half, 7),
        (r1, 9),
        (ra, 10),
        (ra2, 11),
        (zr, 12),
        (nr1, 14),
        (nr2, 16),
        (nr3, 18),
    ]
    for ref, k in sent:
        wait_bytes(ref, sem.at[k])


SCRATCH = [
    pltpu.SMEM((IMG,), jnp.int32),
    pltpu.SMEM((32,), jnp.int32),
    pltpu.SMEM((1,), jnp.int32),
    VMEM((1, C), F32),
    VMEM((SIDE * SIDE, C), F32),
    VMEM((C, E), BF16),
    VMEM((64, E), BF16),
    VMEM((IMG, SIDE, SIDE, C), BF16),
    VMEM((3, 3, C, C), BF16),
    VMEM((3, 3, C, C), BF16),
    VMEM((3, 3, C, C), BF16),
    VMEM((QUEUE, E), BF16),
    VMEM((IMG, TALL, 3 * C), BF16),
    VMEM((IMG, TALL, 3 * C), BF16),
    VMEM((IMG, TALL, 3 * C), BF16),
    VMEM((IMG, TALL, 3 * C), BF16),
    VMEM((C, IMG * 256), BF16),
    VMEM((C, IMG * 256), BF16),
    VMEM((IMG, CELLS, C), F32),
    VMEM((3, CELLS, C), F32),
    VMEM((16, C), F32),
    VMEM((64, E), BF16),
    VMEM((32, E), BF16),
    VMEM((32, E), BF16),
    VMEM((3, 32, E), BF16),
    VMEM((32, E), BF16),
    VMEM((3, 32, E), BF16),
    VMEM((8, 32, E), BF16),
    VMEM((8, 64, E), BF16),
    VMEM((16, 2, 160, C), BF16),
    VMEM((16, 160, C), BF16),
    VMEM((4, 4, 160, 128), BF16),
    VMEM((4, 176, 128), F32),
    VMEM((4, 4, 160, 128), BF16),
    VMEM((6, 4, 160, 128), BF16),
    VMEM((4, 48, 128), F32),
    VMEM((4, 4, 48, 128), BF16),
    VMEM((4, 48, 128), F32),
    VMEM((4, 4, 48, 128), BF16),
    VMEM((6, 4, 48, 128), BF16),
    VMEM((8, 48, 128), F32),
    VMEM((8, 48, 128), BF16),
    VMEM((7, 48, 128), BF16),
    VMEM((3, 8, 128), F32),
    VMEM((15, 8, 128), F32),
    VMEM((7, 8, 128), F32),
    VMEM((1, 8, 128), F32),
    VMEM((1024, 128), F32),
    DMA((11,)),
    DMA((20,)),
    DMA((7,)),
    DMA((4,)),
    DMA((4,)),
    DMA((4,)),
]


def shards(
    images,
    labels,
    conv_one,
    conv_two,
    prelu_slope,
    spatial,
    head_weight,
    class_queue,
    candidates,
    generator,
    offset,
):
    far = pl.BlockSpec(memory_space=pl.ANY)
    near = pl.BlockSpec(memory_space=pltpu.VMEM)
    loss, fresh, update = pl.pallas_call(
        kernel,
        out_shape=(
            VMEM((IMG,), F32),
            VMEM((QUEUE, E), BF16),
            VMEM((2 * CHUNK, 128), F32),
        ),
        in_specs=[far] * 11,
        out_specs=(near, near, near),
        scratch_shapes=SCRATCH,
        name="whole_step",
        compiler_params=pltpu.CompilerParams(
            collective_id=0, has_side_effects=True, vmem_limit_bytes=56 << 20
        ),
    )(
        images,
        labels,
        conv_one,
        conv_two,
        prelu_slope.reshape(1, C),
        spatial,
        head_weight,
        class_queue,
        candidates,
        generator,
        offset,
    )
    return loss, fresh, update.reshape(2 * CHUNK * 128)


def solution(mesh):
    in_specs = (
        P(("dp", "rep"), None, None, None),
        P(("dp", "rep")),
        P(),
        P(),
        P(),
        P(),
        P(),
        P(),
        P(("dp", "rep"), None),
        P(),
        P(),
    )
    out_specs = (P(("dp", "rep")), P(), P(("dp", "rep")))
    return jax.shard_map(
        shards, mesh=mesh, in_specs=in_specs, out_specs=out_specs, check_vma=False
    )
```
